512 devices in a mesh: dp: 64 (over z_lo, y, x), mp: 8 (over z_hi, core).
Axes of the slice: x: 4, y: 4, z: 16 (z_hi: 4, z_lo: 4; z = z_hi * 4 + z_lo), core: 2. Of those that a mesh axis runs over, the one named last changes fastest.
Arguments:
- inputs: bfloat16 [8192, 5120], P('dp', 'mp'), may hold values from -6 to 6
- upstream: bfloat16 [8192, 5120], P('dp', 'mp'), may hold values from -0.796875 to 0.796875
- master: float32 [3, 512, 5120], P(None, 'mp', 'dp'), may hold values from -0.078125 to 0.078125
- moment_one: float32 [3, 512, 5120], P(None, 'mp', 'dp'), may hold values from -6 to 6
- moment_two: float32 [3, 512, 5120], P(None, 'mp', 'dp'), may hold values from 1 to 100
Outputs:
- master_new: float32 [3, 512, 5120], P(None, 'mp', 'dp')
- moment_one_new: float32 [3, 512, 5120], P(None, 'mp', 'dp')
- moment_two_new: float32 [3, 512, 5120], P(None, 'mp', 'dp')
- weights_new: bfloat16 [3, 512, 5120], P(None, 'mp')
The draws below stay inside these ranges and needn't reach their ends.
All inputs are finite; a program needn't handle non-finite values.
Results may differ from the reference program's by a relative error of at most 0.001.
Values may be sent and summed in bfloat16 or wider, within the bound.
A program may use at most 64 MiB of HBM per device.

```python
import math
import jax
import jax.numpy as jnp

D = 5120
TOKENS = 8192
HIDDEN_SIZE = 512


def with_spikes(array, key, source, target, blocks, factor):
    owner, partner = [(jnp.arange(array.shape[dim]) // (array.shape[dim] // blocks)).reshape([-1 if axis == dim else 1 for axis in range(array.ndim)]) for dim in (source, target)]
    chosen = jax.random.permutation(key, blocks)[partner]
    strong = (owner == chosen) | (owner == (partner + blocks // 2) % blocks)
    return jnp.where(strong, factor * array, array)


def block_scale(stream_key, dims, split, smallest, largest):
    loudness = 1.0
    for dim, parts in split:
        draws = jax.random.uniform(jax.random.fold_in(jax.random.fold_in(stream_key, 6), dim), (parts,), jnp.float32, smallest / len(split), largest / len(split))
        loudness = loudness * jnp.repeat(jnp.exp(draws), dims[dim] // parts).reshape((-1,) + (1,) * (len(dims) - 1 - dim))
    return loudness


def normal_values(key, shape, width, reach, pieces=(), held_as=jnp.bfloat16):
    drawn = jax.random.normal(key, shape, jnp.float32) * width
    if len(pieces) > 0:
        drawn = block_scale(key, shape, pieces, -0.22, 0.18) * drawn
    return jnp.clip(drawn, min=-reach, max=reach).astype(held_as)


def gaussian_with(rng, dims, width, most, cuts, heavy, held_as=jnp.bfloat16):
    entries = width * jax.random.normal(rng, dims, jnp.float32)
    if cuts:
        entries = entries * block_scale(rng, dims, cuts, -0.22, 0.18)
    return jnp.clip(with_spikes(entries, jax.random.fold_in(rng, 3), *heavy), -most, most).astype(held_as)


def setup_inputs(seed: int = 0) -> dict:
    seeds = jax.random.split(jax.random.key(seed), 6)
    return {
        "inputs": normal_values(seeds[0], (TOKENS, D), 1.0, 6.0, ((0, 64), (1, 8))),
        "upstream": gaussian_with(seeds[1], (TOKENS, D), 0.1, 0.796875, ((0, 64), (1, 8)), (0, 1, 64, 4.0)),
        "master": normal_values(seeds[2], (3, HIDDEN_SIZE, D), D ** -0.5, 0.078125, ((1, 8), (2, 64)), jnp.float32),
        "moment_one": normal_values(seeds[3], (3, HIDDEN_SIZE, D), 1.0, 6.0, ((1, 8), (2, 64)), jnp.float32),
        "moment_two": jnp.clip(jnp.exp(math.log(100.0) - 4.6051702 * jax.random.uniform(seeds[4], (3, HIDDEN_SIZE, D), jnp.float32) ** block_scale(seeds[4], (3, HIDDEN_SIZE, D), ((1, 8), (2, 64)), -0.2, 0.2)), 1.0, 100.0),
    }


beta_one = 0.9
beta_two = 0.95
learn_rate = 0.0003
decay_rate = 0.1
eps_small = 1e-08
corr_one = 1.0 - 0.9 ** 40
corr_two = 1.0 - 0.95 ** 40

def reference(inputs, upstream, master, moment_one, moment_two):
    weights = master.astype(jnp.bfloat16)
    gate = jnp.dot(inputs, weights[0].T, preferred_element_type=jnp.float32)
    upval = jnp.dot(inputs, weights[1].T, preferred_element_type=jnp.float32)
    sigma = jax.nn.sigmoid(gate)
    hidden = (gate * sigma * upval).astype(jnp.bfloat16)
    dhidden = jnp.dot(upstream, weights[2].T, preferred_element_type=jnp.float32)
    dgate = (dhidden * upval * sigma * (1.0 + gate * (1.0 - sigma))).astype(jnp.bfloat16)
    dup = (dhidden * gate * sigma).astype(jnp.bfloat16)
    grads = jnp.stack([jnp.dot(dgate.T, inputs, preferred_element_type=jnp.float32), jnp.dot(dup.T, inputs, preferred_element_type=jnp.float32), jnp.dot(hidden.T, upstream, preferred_element_type=jnp.float32)])
    first = beta_one * moment_one + (1.0 - beta_one) * grads
    second = beta_two * moment_two + (1.0 - beta_two) * grads * grads
    update = first / corr_one / (jnp.sqrt(second / corr_two) + eps_small)
    master_new = master - learn_rate * (update + decay_rate * master)
    return (master_new, first, second, master_new.astype(jnp.bfloat16))
```

```python
import functools

import jax
import jax.numpy as jnp
from jax import lax
from jax.experimental import pallas as pl
from jax.experimental.pallas import tpu as pltpu
from jax.sharding import PartitionSpec as P

beta_one = 0.9
beta_two = 0.95
learn_rate = 0.0003
decay_rate = 0.1
eps_small = 1e-08
corr_one = 1.0 - 0.9**40
corr_two = 1.0 - 0.95**40

MESH = pl.DeviceIdType.MESH
f32 = jnp.float32
bf16 = jnp.bfloat16
N_COPIES = 64


def kernel(
    stop,
    inputs, upstream, master, moment_one, moment_two,
    master_new, first_new, second_new, weights_new,
    feats, wown, wbuf, part, core_in, quarter, rs_half, rs_full, dcat,
    featT, gbuf, gy_half, gy_full, gline, gz_in, g01, g2, aline, fin,
    send_sems, recv_sems,
):
    i, j = lax.axis_index("dp"), lax.axis_index("mp")
    z, y, x = i // 16, (i // 4) % 4, i % 4
    zh, core = j // 2, j % 2

    def dev(zh=zh, core=core, z=z, y=y, x=x):
        return (z * 16 + y * 4 + x, zh * 2 + core)

    right, left = dev(x=(x + 1) % 4), dev(x=(x + 3) % 4)
    up, down = dev(y=(y + 1) % 4), dev(y=(y + 3) % 4)
    line = [None] + [dev(z=(z + k) % 4) for k in (1, 2, 3)]
    above, below = dev(zh=(zh + 1) % 4), dev(zh=(zh + 3) % 4)
    mate = dev(core=1 - core)
    holder = dev(zh=z, core=y // 2, z=x, y=2 * core + 1 - y % 2, x=zh)
    holder_b = dev(zh=z, core=y // 2, z=x, y=2 * (1 - core) + 1 - y % 2, x=zh)
    owner = dev(zh=x, core=y // 2, z=zh, y=2 * core + 1 - y % 2, x=z)
    owner_b = dev(zh=x, core=1 - y // 2, z=zh, y=2 * core + 1 - y % 2, x=z)
    slot = lambda v: v + 1 - 2 * (v % 2)
    yu, yd, y2 = (y + 1) % 4, (y + 3) % 4, (y + 2) % 4
    zu, zd, z2 = (zh + 1) % 4, (zh + 3) % 4, (zh + 2) % 4

    started = []

    def put(src, dst, to):
        k = len(started)
        copy = pltpu.make_async_remote_copy(
            src_ref=src, dst_ref=dst, send_sem=send_sems.at[k], recv_sem=recv_sems.at[k],
            device_id=to, device_id_type=MESH,
        )
        copy.start()
        started.append(copy)
        return copy

    def finish():
        for copy in started:
            copy.wait_send()

    barrier = pltpu.get_barrier_semaphore()
    greeted = [right, left, up, down, *line[1:], above, below, mate, holder, holder_b, owner, owner_b]
    for other in greeted:
        pl.semaphore_signal(barrier, inc=1, device_id=other, device_id_type=MESH)

    feats[0, 0] = inputs[...]
    feats[1, 0] = upstream[...]
    low = lax.broadcasted_iota(jnp.int32, (80, 128), 1) < 64
    rows = master[...].reshape(192, 80)
    wown[0:80, :] = rows[0:128].T.astype(bf16)
    down_rows = jnp.concatenate([rows[128:192], rows[128:192]], axis=0).T
    wown[80:160, :] = jnp.where(low == (core == 0), down_rows, 0.0).astype(bf16)

    pl.semaphore_wait(barrier, len(greeted))

    c_w = put(wown, wbuf.at[2 * core + y % 2, x], holder)
    c_r = [put(feats.at[n, 0], feats.at[n, 3], right) for n in (0, 1)]
    c_l = [put(feats.at[n, 0], feats.at[n, 1], left) for n in (1, 0)]

    c_w.wait_recv()
    mine = wbuf.at[slot(y), z]
    c_z = [put(mine, mine, line[k]) for k in (1, 2, 3)]
    for c in c_z:
        c.wait_recv()
    mine = wbuf.at[slot(y)]
    c_u = put(mine, mine, up)
    c_d = put(mine, mine, down)
    c_r[0].wait_recv()
    c_r2 = put(feats.at[0, 3], feats.at[0, 2], right)
    c_l[0].wait_recv()
    c_l2 = put(feats.at[1, 1], feats.at[1, 2], left)
    c_u.wait_recv()
    piece = wbuf.at[slot(yd), pl.ds(0, 2)]
    c_u2 = put(piece, piece, up)
    c_d.wait_recv()
    piece = wbuf.at[slot(yu), pl.ds(2, 2)]
    c_d2 = put(piece, piece, down)
    for c in (c_r[1], c_l[1], c_r2, c_l2, c_u2, c_d2):
        c.wait_recv()
    if stop == 1:
        return finish()

    w01 = [wbuf[2 * b : 2 * b + 2, :, 0:80, :].reshape(640, 128) for b in (0, 1)]
    w01 = jnp.concatenate(w01, axis=1)
    w2 = (wbuf[0:2, :, 80:160, :] + wbuf[2:4, :, 80:160, :]).reshape(640, 128)
    for half in (0, 1):
        a = feats[0, 2 * half : 2 * half + 2].reshape(256, 640)
        u = feats[1, 2 * half : 2 * half + 2].reshape(256, 640)
        part[half, :, 0:256] = jnp.dot(a, w01, preferred_element_type=f32)
        part[half, :, 256:384] = jnp.dot(u, w2, preferred_element_type=f32)

    c_m = put(part.at[1 - core], core_in, mate)
    for n in (0, 1):
        featT[n] = feats[n].reshape(512, 640).T
    c_m.wait_recv()
    quarter[...] = (part[core] + core_in[...]).reshape(4, 64, 384)
    lo, hi = pl.ds(0, 32), pl.ds(32, 32)
    c_a1 = put(quarter.at[z2, lo], rs_half.at[0], above)
    c_b1 = put(quarter.at[z2, hi], rs_half.at[1], below)
    c_a2 = put(quarter.at[zu, hi], rs_full.at[0, hi], above)
    c_b2 = put(quarter.at[zd, lo], rs_full.at[1, lo], below)
    c_a1.wait_recv()
    quarter[zu, 0:32] += rs_half[0]
    c_a3 = put(quarter.at[zu, lo], rs_full.at[0, lo], above)
    c_b1.wait_recv()
    quarter[zd, 32:64] += rs_half[1]
    c_b3 = put(quarter.at[zd, hi], rs_full.at[1, hi], below)
    for c in (c_a2, c_b2, c_a3, c_b3):
        c.wait_recv()
    if stop == 2:
        return finish()

    total = quarter[zh] + rs_full[0] + rs_full[1]
    t0, t1, dhidden = total[:, 0:128], total[:, 128:256], total[:, 256:384]
    low = lax.broadcasted_iota(jnp.int32, (64, 128), 1) < 64
    gate = jnp.where(low, t0, pltpu.roll(t1, 64, 1))
    upval = jnp.where(low, pltpu.roll(t0, 64, 1), t1)
    sigma = jax.nn.sigmoid(gate)
    hidden = gate * sigma * upval
    dgate = dhidden * upval * sigma * (1.0 + gate * (1.0 - sigma))
    dup = dhidden * gate * sigma
    dcat[core, zh, :, 0:128] = jnp.where(low, dgate, pltpu.roll(dup, 64, 1)).astype(bf16)
    dcat[core, zh, :, 128:256] = jnp.where(low, pltpu.roll(dgate, 64, 1), dup).astype(bf16)
    dcat[core, zh, :, 256:384] = hidden.astype(bf16)

    mine = dcat.at[core, zh]
    c_a = put(mine, mine, above)
    c_b = put(mine, mine, below)
    c_m = [put(mine, mine, mate)]
    c_a.wait_recv()
    piece = dcat.at[core, zd, lo]
    c_a2 = put(piece, piece, above)
    c_b.wait_recv()
    piece = dcat.at[core, zu, hi]
    c_b2 = put(piece, piece, below)
    for v in (zd, zu):
        piece = dcat.at[core, v]
        c_m.append(put(piece, piece, mate))
    c_a2.wait_recv()
    c_b2.wait_recv()
    piece = dcat.at[core, z2]
    c_m.append(put(piece, piece, mate))
    for c in c_m:
        c.wait_recv()
    if stop == 3:
        return finish()

    d01 = dcat[:, :, :, 0:256].reshape(512, 256)
    d2 = dcat[:, :, :, 256:384].reshape(512, 128)
    for s in range(8):
        span = slice(80 * s, 80 * s + 80)
        p01 = jnp.dot(featT[0, span, :], d01, preferred_element_type=f32)
        p2 = jnp.dot(featT[1, span, :], d2, preferred_element_type=f32)
        for b in (0, 1):
            gbuf[2 * b + s // 4, s % 4, 0:80, :] = p01[:, 128 * b : 128 * b + 128]
            gbuf[2 * b + s // 4, s % 4, 80:120, :] = p2[40 * b : 40 * b + 40]

    lo, hi = pl.ds(0, 2), pl.ds(2, 2)
    c_a1 = put(gbuf.at[slot(y2), lo], gy_half.at[0], up)
    c_b1 = put(gbuf.at[slot(y2), hi], gy_half.at[1], down)
    c_a2 = put(gbuf.at[slot(yu), hi], gy_full.at[0, hi], up)
    c_b2 = put(gbuf.at[slot(yd), lo], gy_full.at[1, lo], down)
    c_a1.wait_recv()
    gbuf[slot(yu), 0:2] += gy_half[0]
    c_a3 = put(gbuf.at[slot(yu), lo], gy_full.at[0, lo], up)
    c_b1.wait_recv()
    gbuf[slot(yd), 2:4] += gy_half[1]
    c_b3 = put(gbuf.at[slot(yd), hi], gy_full.at[1, hi], down)
    for c in (c_a2, c_b2, c_a3, c_b3):
        c.wait_recv()
    if stop == 4:
        return finish()
    gline[...] = gbuf[slot(y)] + gy_full[0] + gy_full[1]
    c_z = [put(gline.at[(z + k) % 4], gz_in.at[k - 1], line[k]) for k in (1, 2, 3)]
    for c in c_z:
        c.wait_recv()
    gline[z] += gz_in[0] + gz_in[1] + gz_in[2]
    if stop == 5:
        return finish()

    c_1 = put(gline.at[z, pl.ds(0, 80)], g01, owner)
    c_2 = put(gline.at[z, pl.ds(80, 40)], g2.at[y // 2], owner)
    c_3 = put(gline.at[z, pl.ds(80, 40)], g2.at[y // 2], owner_b)
    for c in (c_1, c_2, c_3):
        c.wait_recv()
    if stop == 6:
        return finish()

    down_grads = g2[...].reshape(80, 128).T
    down_grads = jnp.where(core == 0, down_grads[0:64], down_grads[64:128])
    grads = jnp.concatenate([g01[...].T, down_grads], axis=0).reshape(3, 64, 80)
    first = beta_one * moment_one[...] + (1.0 - beta_one) * grads
    second = beta_two * moment_two[...] + (1.0 - beta_two) * grads * grads
    update = first / corr_one / (jnp.sqrt(second / corr_two) + eps_small)
    fresh = master[...] - learn_rate * (update + decay_rate * master[...])
    first_new[...] = first
    second_new[...] = second
    master_new[...] = fresh
    fresh = fresh.reshape(192, 80)
    aline[z, 0:80, :] = fresh[0:128].T.astype(bf16)
    down_rows = jnp.concatenate([fresh[128:192], jnp.zeros((64, 80), f32)], axis=0).T
    aline[z, 80:160, :] = down_rows.astype(bf16)

    mine = aline.at[z]
    c_z = [put(mine, mine, line[k]) for k in (1, 2, 3)]
    for c in c_z:
        c.wait_recv()
    fin[y, x, 0:320, :] = aline[:, 0:80, :].reshape(320, 128)
    tail = aline[:, 80:160, :].astype(f32)
    packed = tail[0:2].reshape(160, 128) + pltpu.roll(tail[2:4].reshape(160, 128), 64, 1)
    fin[y, x, 320:480, :] = packed.astype(bf16)
    if stop == 7:
        return finish()

    xu, xd = (x + 1) % 4, (x + 3) % 4
    a_all, b_all = pl.ds(0, 240), pl.ds(240, 240)
    mine_a, mine_b = fin.at[y, x, a_all], fin.at[y, x, b_all]
    c_ar, c_al = put(mine_a, mine_a, right), put(mine_a, mine_a, left)
    c_bu, c_bd = put(mine_b, mine_b, up), put(mine_b, mine_b, down)
    c_ar.wait_recv()
    piece = fin.at[y, xd, pl.ds(0, 128)]
    c_ar2 = put(piece, piece, right)
    c_al.wait_recv()
    piece = fin.at[y, xu, pl.ds(128, 112)]
    c_al2 = put(piece, piece, left)
    c_bu.wait_recv()
    piece = fin.at[yd, x, pl.ds(240, 128)]
    c_bu2 = put(piece, piece, up)
    c_bd.wait_recv()
    piece = fin.at[yu, x, pl.ds(368, 112)]
    c_bd2 = put(piece, piece, down)
    for c in (c_ar2, c_al2, c_bu2, c_bd2):
        c.wait_recv()
    if stop == 8:
        return finish()
    mine_a, mine_b = fin.at[y, :, a_all], fin.at[:, x, b_all]
    c_au, c_ad = put(mine_a, mine_a, up), put(mine_a, mine_a, down)
    c_br, c_bl = put(mine_b, mine_b, right), put(mine_b, mine_b, left)
    c_au.wait_recv()
    piece = fin.at[yd, pl.ds(0, 2), a_all]
    c_au2 = put(piece, piece, up)
    c_br.wait_recv()
    piece = fin.at[pl.ds(0, 2), xd, b_all]
    c_br2 = put(piece, piece, right)
    c_ad.wait_recv()
    piece = fin.at[yu, pl.ds(2, 2), a_all]
    c_ad2 = put(piece, piece, down)
    c_bl.wait_recv()
    piece = fin.at[pl.ds(2, 2), xu, b_all]
    c_bl2 = put(piece, piece, left)
    for c in (c_au2, c_ad2, c_br2, c_bl2):
        c.wait_recv()
    if stop == 9:
        return finish()

    for n in range(4):
        cols = slice(1280 * n, 1280 * n + 1280)
        block = fin[:, :, 80 * n : 80 * n + 80, :].reshape(1280, 128).T
        weights_new[0, :, cols] = block[0:64]
        weights_new[1, :, cols] = block[64:128]
    for n in range(2):
        block = fin[:, :, 320 + 80 * n : 400 + 80 * n, :].reshape(1280, 128).T
        weights_new[2, :, 1280 * n : 1280 * n + 1280] = block[0:64]
        weights_new[2, :, 1280 * (n + 2) : 1280 * (n + 3)] = block[64:128]
    finish()


def local(stop, inputs, upstream, master, moment_one, moment_two):
    shard = jax.ShapeDtypeStruct((3, 64, 80), f32)
    vmem = pl.BlockSpec(memory_space=pltpu.VMEM)
    return pl.pallas_call(
        functools.partial(kernel, stop),
        out_shape=(shard, shard, shard, jax.ShapeDtypeStruct((3, 64, 5120), bf16)),
        in_specs=[vmem] * 5,
        out_specs=(vmem,) * 4,
        scratch_shapes=[
            pltpu.VMEM((2, 4, 128, 640), bf16),
            pltpu.VMEM((160, 128), bf16),
            pltpu.VMEM((4, 4, 160, 128), bf16),
            pltpu.VMEM((2, 256, 384), f32),
            pltpu.VMEM((256, 384), f32),
            pltpu.VMEM((4, 64, 384), f32),
            pltpu.VMEM((2, 32, 384), f32),
            pltpu.VMEM((2, 64, 384), f32),
            pltpu.VMEM((2, 4, 64, 384), bf16),
            pltpu.VMEM((2, 640, 512), bf16),
            pltpu.VMEM((4, 4, 120, 128), f32),
            pltpu.VMEM((2, 2, 120, 128), f32),
            pltpu.VMEM((2, 4, 120, 128), f32),
            pltpu.VMEM((4, 120, 128), f32),
            pltpu.VMEM((3, 120, 128), f32),
            pltpu.VMEM((80, 128), f32),
            pltpu.VMEM((2, 40, 128), f32),
            pltpu.VMEM((4, 160, 128), bf16),
            pltpu.VMEM((4, 4, 480, 128), bf16),
            pltpu.SemaphoreType.DMA((N_COPIES,)),
            pltpu.SemaphoreType.DMA((N_COPIES,)),
        ],
        compiler_params=pltpu.CompilerParams(
            collective_id=0, has_side_effects=True, vmem_limit_bytes=40 * 2**20
        ),
        cost_estimate=pl.CostEstimate(
            flops=503316480, bytes_accessed=8000000, transcendentals=8192
        ),
        name="fused_step",
    )(inputs, upstream, master, moment_one, moment_two)


def solution(mesh, stop=0):
    owned = P(None, "mp", "dp")
    return jax.shard_map(
        functools.partial(local, stop),
        mesh=mesh,
        in_specs=(P("dp", "mp"), P("dp", "mp"), owned, owned, owned),
        out_specs=(owned, owned, owned, P(None, "mp", None)),
        check_vma=False,
    )
```

```python
import functools

import jax
import jax.numpy as jnp
from jax import lax
from jax.experimental import pallas as pl
from jax.experimental.pallas import tpu as pltpu
from jax.sharding import PartitionSpec as P

beta_one = 0.9
beta_two = 0.95
learn_rate = 0.0003
decay_rate = 0.1
eps_small = 1e-08
corr_one = 1.0 - 0.9**40
corr_two = 1.0 - 0.95**40

MESH = pl.DeviceIdType.MESH
f32 = jnp.float32
bf16 = jnp.bfloat16
N_COPIES = 96


def kernel(
    stop,
    inputs_hbm, upstream_hbm, master_hbm, moment_one_hbm, moment_two_hbm,
    master_out, first_out, second_out, weights_out,
    feats, state, fresh_state, wown, wbuf, quarter, rs_half, rs_full, dcat,
    featT, gbuf, gy_half, gy_full, gline, gz_in, gin, fin, rows_new,
    send_sems, recv_sems, load_sems, store_sems,
):
    i, j = lax.axis_index("dp"), lax.axis_index("mp")
    z, y, x = i // 16, (i // 4) % 4, i % 4
    zh, core = j // 2, j % 2

    def dev(zh=zh, core=core, z=z, y=y, x=x):
        return (z * 16 + y * 4 + x, zh * 2 + core)

    flip = lambda v: v + 1 - 2 * (v % 2)
    xu, xd, x2 = (x + 1) % 4, (x + 3) % 4, (x + 2) % 4
    yu, yd, y2 = (y + 1) % 4, (y + 3) % 4, (y + 2) % 4
    zu, zd, z2 = (zh + 1) % 4, (zh + 3) % 4, (zh + 2) % 4
    right, left, up, down = dev(x=xu), dev(x=xd), dev(y=yu), dev(y=yd)
    line = [dev(z=(z + k) % 4) for k in (1, 2, 3)]
    skew = [dev(z=(z + k) % 4, x=(x + k) % 4) for k in (1, 2, 3)]
    above, below = dev(zh=zu), dev(zh=zd)
    mate = dev(core=1 - core)
    holder = dev(zh=z, z=x, y=flip(y), x=(zh + x) % 4)
    owner = dev(zh=(x + 4 - z) % 4, z=zh, y=flip(y), x=z)

    started = []

    def put(src, dst, to):
        k = len(started)
        copy = pltpu.make_async_remote_copy(
            src_ref=src, dst_ref=dst, send_sem=send_sems.at[k], recv_sem=recv_sems.at[k],
            device_id=to, device_id_type=MESH,
        )
        copy.start()
        started.append(copy)
        return copy

    def share(ref, to):
        return put(ref, ref, to)

    def arrived(*copies):
        for copy in copies:
            copy.wait_recv()

    def finish():
        for copy in started:
            copy.wait_send()

    barrier = pltpu.get_barrier_semaphore()
    greeted = [right, left, up, down, *line, *skew, above, below, mate, holder, owner]
    for other in greeted:
        pl.semaphore_signal(barrier, inc=1, device_id=other, device_id_type=MESH)

    loads = [
        pltpu.make_async_copy(src, dst, load_sems.at[k])
        for k, (src, dst) in enumerate([
            (master_hbm, state.at[0]),
            (inputs_hbm, feats.at[0, 0, core]),
            (upstream_hbm, feats.at[1, 0, core]),
            (moment_one_hbm, state.at[1]),
            (moment_two_hbm, state.at[2]),
        ])
    ]
    for load in loads:
        load.start()

    def low_lanes(n):
        return lax.broadcasted_iota(jnp.int32, (n, 128), 1) < 64

    def shard_block(rows):
        down_cols = jnp.concatenate([rows[128:192], jnp.zeros((64, 80), f32)], axis=0).T
        rest = jnp.concatenate([down_cols[48:80], jnp.zeros((16, 128), f32)], axis=0)
        folded = down_cols[0:48] + pltpu.roll(rest, 64, 1)
        return jnp.concatenate([rows[0:128].T, folded], axis=0).astype(bf16)

    loads[0].wait()
    wown[...] = shard_block(state[0].reshape(192, 80))
    for load in loads[1:]:
        load.wait()

    pl.semaphore_wait(barrier, len(greeted))

    c_w = put(wown, wbuf.at[y, x], holder)
    own = [feats.at[n, 0, core] for n in (0, 1)]
    c_r = [put(own[n], feats.at[n, 3, core], right) for n in (0, 1)]
    c_l = [put(own[n], feats.at[n, 1, core], left) for n in (1, 0)]
    c_m = [share(own[n], mate) for n in (0, 1)]
    arrived(c_w)
    if stop == 1:
        arrived(*c_r, *c_l, *c_m)
        return finish()
    mine = wbuf.at[flip(y), z]
    c_z = [share(mine, to) for to in skew]
    arrived(c_r[0])
    c_r2 = put(feats.at[0, 3, core], feats.at[0, 2, core], right)
    c_m.append(share(feats.at[0, 3, core], mate))
    arrived(c_l[0])
    c_l2 = put(feats.at[1, 1, core], feats.at[1, 2, core], left)
    c_m.append(share(feats.at[1, 1, core], mate))
    arrived(*c_z)
    if stop == 2:
        arrived(c_r[1], c_l[1], c_r2, c_l2, *c_m)
        return finish()
    mine = wbuf.at[flip(y)]
    c_u, c_d = share(mine, up), share(mine, down)
    arrived(c_r[1])
    c_m.append(share(feats.at[1, 3, core], mate))
    arrived(c_l[1])
    c_m.append(share(feats.at[0, 1, core], mate))
    arrived(c_u)
    c_u2 = share(wbuf.at[flip(yd), pl.ds(0, 2)], up)
    arrived(c_d)
    c_d2 = share(wbuf.at[flip(yu), pl.ds(2, 2)], down)
    arrived(c_r2)
    c_m.append(share(feats.at[0, 2, core], mate))
    arrived(c_l2)
    c_m.append(share(feats.at[1, 2, core], mate))
    arrived(*c_m, c_u2, c_d2)
    if stop == 3:
        return finish()

    w01 = wbuf[:, :, 0:80, :].reshape(1280, 128)
    folded = wbuf[:, :, 80:128, :].reshape(768, 128).astype(f32)
    low = low_lanes(768)
    first_rows = jnp.where(low, folded, 0.0).astype(bf16).reshape(16, 48, 128)
    last_rows = jnp.where(low, pltpu.roll(folded, 64, 1), 0.0).astype(bf16).reshape(16, 48, 128)
    w2 = jnp.concatenate([first_rows, last_rows[:, 0:32]], axis=1).reshape(1280, 128)
    w01 = (w01[0:640], w01[640:1280])
    w2 = (w2[0:640], w2[640:1280])

    def forward(q):
        p01 = jnp.dot(feats[0, q, 0], w01[0], preferred_element_type=f32)
        p01 += jnp.dot(feats[0, q, 1], w01[1], preferred_element_type=f32)
        p2 = jnp.dot(feats[1, q, 0], w2[0], preferred_element_type=f32)
        p2 += jnp.dot(feats[1, q, 1], w2[1], preferred_element_type=f32)
        quarter[q, 0:128] = p01
        quarter[q, 128:192] = p2[0:64] + pltpu.roll(p2[64:128], 64, 1)

    lo, hi = pl.ds(0, 96), pl.ds(96, 96)
    forward(z2)
    c_a1 = put(quarter.at[z2, lo], rs_half.at[0], above)
    c_b1 = put(quarter.at[z2, hi], rs_half.at[1], below)
    forward(zu)
    c_a2 = put(quarter.at[zu, hi], rs_full.at[0, hi], above)
    forward(zd)
    c_b2 = put(quarter.at[zd, lo], rs_full.at[1, lo], below)
    forward(zh)
    arrived(c_a1)
    quarter[zu, 0:96] += rs_half[0]
    c_a3 = put(quarter.at[zu, lo], rs_full.at[0, lo], above)
    arrived(c_b1)
    quarter[zd, 96:192] += rs_half[1]
    c_b3 = put(quarter.at[zd, hi], rs_full.at[1, hi], below)
    for n in (0, 1):
        for q in range(4):
            for d in (0, 1):
                block = feats[n, q, d].T.reshape(2, 320, 128)
                featT[n, 2 * d : 2 * d + 2, :, 128 * q : 128 * q + 128] = block
    arrived(c_a2, c_b2, c_a3, c_b3)
    if stop == 4:
        return finish()

    total = quarter[zh] + rs_full[0] + rs_full[1]
    gate = total[0:128]
    upval = pltpu.roll(gate, 64, 1)
    dhidden = jnp.concatenate([total[128:192], pltpu.roll(total[128:192], 64, 1)], axis=0)
    sigma = jax.nn.sigmoid(gate)
    hidden = gate * sigma * upval
    dgate = dhidden * upval * sigma * (1.0 + gate * (1.0 - sigma))
    dup = dhidden * gate * sigma
    low = low_lanes(128)
    dcat[zh, 0:128] = jnp.where(low, dgate, pltpu.roll(dup, 64, 1)).astype(bf16)
    hidden = jnp.where(low[0:64], hidden[0:64], pltpu.roll(hidden[64:128], 64, 1))
    dcat[zh, 128:192] = hidden.astype(bf16)

    c_a1, c_b1 = share(dcat.at[zh, lo], above), share(dcat.at[zh, hi], below)
    c_a2, c_b2 = share(dcat.at[zh, hi], above), share(dcat.at[zh, lo], below)
    arrived(c_a1)
    c_a3 = share(dcat.at[zd, lo], above)
    arrived(c_b1)
    c_b3 = share(dcat.at[zu, hi], below)
    arrived(c_a2, c_b2, c_a3, c_b3)
    if stop == 5:
        return finish()

    d01 = dcat[:, 0:128, :].reshape(512, 128)
    low = low_lanes(256)
    folded = dcat[:, 128:192, :].reshape(256, 128).astype(f32)
    early = jnp.where(low, folded, 0.0).astype(bf16).reshape(4, 64, 128)
    late = jnp.where(low, pltpu.roll(folded, 64, 1), 0.0).astype(bf16).reshape(4, 64, 128)
    d2 = jnp.concatenate([early, late], axis=1).reshape(512, 128)

    def backward(v):
        p01 = jnp.dot(featT[0, v], d01, preferred_element_type=f32)
        p2 = jnp.dot(featT[1, v], d2, preferred_element_type=f32).reshape(4, 80, 128)
        rest = pltpu.roll(p2[:, 40:80].reshape(160, 128), 64, 1).reshape(4, 40, 128)
        gbuf[v, :, 0:80] = p01.reshape(4, 80, 128)
        gbuf[v, :, 80:120] = p2[:, 0:40] + rest

    lo, hi = pl.ds(0, 2), pl.ds(2, 2)
    backward(flip(y2))
    c_a1 = put(gbuf.at[flip(y2), lo], gy_half.at[0], up)
    c_b1 = put(gbuf.at[flip(y2), hi], gy_half.at[1], down)
    backward(flip(yu))
    c_a2 = put(gbuf.at[flip(yu), hi], gy_full.at[0, hi], up)
    backward(flip(yd))
    c_b2 = put(gbuf.at[flip(yd), lo], gy_full.at[1, lo], down)
    backward(flip(y))
    arrived(c_a1)
    gbuf[flip(yu), 0:2] += gy_half[0]
    c_a3 = put(gbuf.at[flip(yu), lo], gy_full.at[0, lo], up)
    arrived(c_b1)
    gbuf[flip(yd), 2:4] += gy_half[1]
    c_b3 = put(gbuf.at[flip(yd), hi], gy_full.at[1, hi], down)
    arrived(c_a2, c_b2, c_a3, c_b3)
    gline[...] = gbuf[flip(y)] + gy_full[0] + gy_full[1]
    if stop == 6:
        return finish()
    c_z = [put(gline.at[(z + k) % 4], gz_in.at[k - 1], skew[k - 1]) for k in (1, 2, 3)]
    arrived(*c_z)
    gline[z] += gz_in[0] + gz_in[1] + gz_in[2]
    if stop == 7:
        return finish()

    arrived(put(gline.at[z], gin, owner))
    if stop == 8:
        return finish()

    g01 = gin[0:80]
    g2 = jnp.concatenate([gin[80:120], pltpu.roll(gin[80:120], 64, 1)], axis=0)
    grads = jnp.concatenate([g01.T, g2.T[0:64]], axis=0).reshape(3, 64, 80)
    master, moment_one, moment_two = state[0], state[1], state[2]
    first = beta_one * moment_one + (1.0 - beta_one) * grads
    second = beta_two * moment_two + (1.0 - beta_two) * grads * grads
    update = first / corr_one / (jnp.sqrt(second / corr_two) + eps_small)
    fresh = master - learn_rate * (update + decay_rate * master)
    fin[y, x, z] = shard_block(fresh.reshape(192, 80))

    c_z = [share(fin.at[y, x, z], to) for to in line]
    fresh_state[0] = fresh
    fresh_state[1] = first
    fresh_state[2] = second
    stores = [
        pltpu.make_async_copy(fresh_state.at[k], out, store_sems.at[k])
        for k, out in enumerate((master_out, first_out, second_out))
    ]
    for store in stores:
        store.start()
    arrived(*c_z)
    if stop == 9:
        for store in stores:
            store.wait()
        return finish()

    mine = fin.at[y, x]
    c_r, c_l, c_u, c_d = (share(mine, to) for to in (right, left, up, down))
    a, b = pl.ds(0, 2), pl.ds(2, 2)
    part = lambda yy, xx, s: fin.at[yy, xx, s]
    arrived(c_r)
    c_ax = [share(part(y, xd, 0), right)]
    ay1 = [share(part(y, xd, a), up), share(part(y, xd, a), down)]
    arrived(c_l)
    c_ax.append(share(part(y, xu, 1), left))
    ay2 = [share(part(y, xu, a), up), share(part(y, xu, a), down)]
    arrived(c_u)
    c_by = [share(part(yd, x, 2), up)]
    bx1 = [share(part(yd, x, b), right), share(part(yd, x, b), left)]
    arrived(c_d)
    c_by.append(share(part(yu, x, 3), down))
    bx2 = [share(part(yu, x, b), right), share(part(yu, x, b), left)]
    last = [
        share(part(yd, x, 0), up), share(part(yu, x, 1), down),
        share(part(y, xd, 2), right), share(part(y, xu, 3), left),
    ]
    arrived(*c_ax)
    ay3 = [share(part(y, x2, a), up), share(part(y, x2, a), down)]
    arrived(*c_by)
    bx3 = [share(part(y2, x, b), right), share(part(y2, x, b), left)]
    for va, vb, ca, cb in ((xd, yd, ay1, bx1), (xu, yu, ay2, bx2), (x2, y2, ay3, bx3)):
        arrived(ca[0])
        last.append(share(part(yd, va, 0), up))
        arrived(ca[1])
        last.append(share(part(yu, va, 1), down))
        arrived(cb[0])
        last.append(share(part(vb, xd, 2), right))
        arrived(cb[1])
        last.append(share(part(vb, xu, 3), left))
    arrived(*last)
    if stop == 10:
        for store in stores:
            store.wait()
        return finish()

    low = low_lanes(768)
    for n in range(4):
        cols = slice(1280 * n, 1280 * n + 1280)
        both = fin[:, :, n, 0:80, :].reshape(1280, 128).T
        rows_new[0, :, cols] = both[0:64]
        rows_new[1, :, cols] = both[64:128]
        folded = fin[:, :, n, 80:128, :].reshape(768, 128).astype(f32)
        rest = pltpu.roll(folded, 64, 1).reshape(16, 48, 128)[:, 0:32]
        third = jnp.concatenate([folded.reshape(16, 48, 128), rest], axis=1)
        rows_new[2, :, cols] = third.reshape(1280, 128).astype(bf16).T[0:64]
        store = pltpu.make_async_copy(
            rows_new.at[:, :, pl.ds(1280 * n, 1280)],
            weights_out.at[:, :, pl.ds(1280 * n, 1280)],
            store_sems.at[3 + n],
        )
        store.start()
        stores.append(store)
    for store in stores:
        store.wait()
    finish()


def local(stop, inputs, upstream, master, moment_one, moment_two):
    shard = jax.ShapeDtypeStruct((3, 64, 80), f32)
    hbm = pl.BlockSpec(memory_space=pltpu.HBM)
    return pl.pallas_call(
        functools.partial(kernel, stop),
        out_shape=(shard, shard, shard, jax.ShapeDtypeStruct((3, 64, 5120), bf16)),
        in_specs=[hbm] * 5,
        out_specs=(hbm,) * 4,
        scratch_shapes=[
            pltpu.VMEM((2, 4, 2, 128, 640), bf16),
            pltpu.VMEM((3, 3, 64, 80), f32),
            pltpu.VMEM((3, 3, 64, 80), f32),
            pltpu.VMEM((128, 128), bf16),
            pltpu.VMEM((4, 4, 128, 128), bf16),
            pltpu.VMEM((4, 192, 128), f32),
            pltpu.VMEM((2, 96, 128), f32),
            pltpu.VMEM((2, 192, 128), f32),
            pltpu.VMEM((4, 192, 128), bf16),
            pltpu.VMEM((2, 4, 320, 512), bf16),
            pltpu.VMEM((4, 4, 120, 128), f32),
            pltpu.VMEM((2, 2, 120, 128), f32),
            pltpu.VMEM((2, 4, 120, 128), f32),
            pltpu.VMEM((4, 120, 128), f32),
            pltpu.VMEM((3, 120, 128), f32),
            pltpu.VMEM((120, 128), f32),
            pltpu.VMEM((4, 4, 4, 128, 128), bf16),
            pltpu.VMEM((3, 64, 5120), bf16),
            pltpu.SemaphoreType.DMA((N_COPIES,)),
            pltpu.SemaphoreType.DMA((N_COPIES,)),
            pltpu.SemaphoreType.DMA((5,)),
            pltpu.SemaphoreType.DMA((7,)),
        ],
        compiler_params=pltpu.CompilerParams(
            collective_id=0, has_side_effects=True, vmem_limit_bytes=40 * 2**20
        ),
        cost_estimate=pl.CostEstimate(
            flops=503316480, bytes_accessed=8000000, transcendentals=8192
        ),
        name="fused_step",
    )(inputs, upstream, master, moment_one, moment_two)


def solution(mesh, stop=0):
    owned = P(None, "mp", "dp")
    return jax.shard_map(
        functools.partial(local, stop),
        mesh=mesh,
        in_specs=(P("dp", "mp"), P("dp", "mp"), owned, owned, owned),
        out_specs=(owned, owned, owned, P(None, "mp", None)),
        check_vma=False,
    )
```

```python
import functools

import jax
import jax.numpy as jnp
from jax import lax
from jax.experimental import pallas as pl
from jax.experimental.pallas import tpu as pltpu
from jax.sharding import PartitionSpec as P

beta_one = 0.9
beta_two = 0.95
learn_rate = 0.0003
decay_rate = 0.1
eps_small = 1e-08
corr_one = 1.0 - 0.9**40
corr_two = 1.0 - 0.95**40

MESH = pl.DeviceIdType.MESH
f32 = jnp.float32
bf16 = jnp.bfloat16
N_COPIES = 128


def adamw(grads, master, moment_one, moment_two):
    first = beta_one * moment_one + (1.0 - beta_one) * grads
    second = beta_two * moment_two + (1.0 - beta_two) * grads * grads
    update = first / corr_one / (jnp.sqrt(second / corr_two) + eps_small)
    return first, second, master - learn_rate * (update + decay_rate * master)


def kernel(
    stop,
    inputs_hbm, upstream_hbm, master_hbm, moment_one_hbm, moment_two_hbm,
    grads_out, weights_out,
    feats, state, grads_own, wown, wbuf, quarter, rs_half, rs_full, dcat,
    featT, gbuf, gy_half, gy_full, gline, gz_in, gin, fin, rows_new,
    send_sems, recv_sems, load_sems, store_sems,
):
    i, j = lax.axis_index("dp"), lax.axis_index("mp")
    z, y, x = i // 16, (i // 4) % 4, i % 4
    zh, core = j // 2, j % 2

    def dev(zh=zh, core=core, z=z, y=y, x=x):
        return (z * 16 + y * 4 + x, zh * 2 + core)

    flip = lambda v: v + 1 - 2 * (v % 2)
    xu, xd, x2 = (x + 1) % 4, (x + 3) % 4, (x + 2) % 4
    yu, yd, y2 = (y + 1) % 4, (y + 3) % 4, (y + 2) % 4
    zu, zd, z2 = (zh + 1) % 4, (zh + 3) % 4, (zh + 2) % 4
    right, left, up, down = dev(x=xu), dev(x=xd), dev(y=yu), dev(y=yd)
    across_x, across_y = dev(x=x2), dev(y=y2)
    line = [dev(z=(z + k) % 4) for k in (1, 2, 3)]
    skew = [dev(z=(z + k) % 4, x=(x + k) % 4) for k in (1, 2, 3)]
    above, below = dev(zh=zu), dev(zh=zd)
    mate = dev(core=1 - core)
    holders = [
        dev(zh=z, z=(x + m) % 4, y=flip(y), x=(zh + x + m) % 4) for m in range(4)
    ]
    owners = [
        dev(zh=(x + 4 - z) % 4, z=zh, y=flip(y), x=(z + 4 - m) % 4) for m in range(4)
    ]

    started = []

    def put(src, dst, to):
        k = len(started)
        copy = pltpu.make_async_remote_copy(
            src_ref=src, dst_ref=dst, send_sem=send_sems.at[k], recv_sem=recv_sems.at[k],
            device_id=to, device_id_type=MESH,
        )
        copy.start()
        started.append(copy)
        return copy

    def share(ref, to):
        return put(ref, ref, to)

    def arrived(*copies):
        for copy in copies:
            copy.wait_recv()

    def finish():
        for copy in started:
            copy.wait_send()

    barrier = pltpu.get_barrier_semaphore()
    greeted = [
        *holders, *owners, above, below, *line, *skew,
        right, left, up, down, across_x, across_y, mate,
    ]
    for other in greeted:
        pl.semaphore_signal(barrier, inc=1, device_id=other, device_id_type=MESH)

    loads = [
        pltpu.make_async_copy(src, dst, load_sems.at[k])
        for k, (src, dst) in enumerate([
            (master_hbm, state.at[0]),
            (inputs_hbm, feats.at[0, 0, core]),
            (upstream_hbm, feats.at[1, 0, core]),
            (moment_one_hbm, state.at[1]),
            (moment_two_hbm, state.at[2]),
        ])
    ]
    for load in loads:
        load.start()

    def low_lanes(n):
        return lax.broadcasted_iota(jnp.int32, (n, 128), 1) < 64

    def shard_block(rows):
        down_cols = jnp.concatenate([rows[128:192], jnp.zeros((64, 80), f32)], axis=0).T
        rest = jnp.concatenate([down_cols[48:80], jnp.zeros((16, 128), f32)], axis=0)
        folded = down_cols[0:48] + pltpu.roll(rest, 64, 1)
        return jnp.concatenate([rows[0:128].T, folded], axis=0).astype(bf16)

    loads[0].wait()
    wown[...] = shard_block(state[0].reshape(192, 80))
    for load in loads[1:]:
        load.wait()

    pl.semaphore_wait(barrier, len(greeted))

    c_w = [put(wown, wbuf.at[y, x], to) for to in holders]
    own = [feats.at[n, 0, core] for n in (0, 1)]
    c_r = [put(own[n], feats.at[n, 3, core], right) for n in (0, 1)]
    c_l = [put(own[n], feats.at[n, 1, core], left) for n in (1, 0)]
    c_m = [share(own[n], mate) for n in (0, 1)]
    c_y = []

    def spread(m):
        arrived(c_w[m])
        piece = wbuf.at[flip(y), (z + 4 - m) % 4]
        c_y.extend(share(piece, to) for to in (up, down, across_y))

    spread(0)
    spread(1)
    arrived(c_r[0])
    c_r2 = put(feats.at[0, 3, core], feats.at[0, 2, core], right)
    arrived(c_l[0])
    c_l2 = put(feats.at[1, 1, core], feats.at[1, 2, core], left)
    spread(2)
    spread(3)
    if stop == 1:
        arrived(*c_y, c_r[1], c_l[1], c_r2, c_l2, *c_m)
        return finish()
    c_m.append(share(feats.at[0, 3, core], mate))
    c_m.append(share(feats.at[1, 1, core], mate))
    arrived(c_r[1])
    c_m.append(share(feats.at[1, 3, core], mate))
    arrived(c_l[1])
    c_m.append(share(feats.at[0, 1, core], mate))
    arrived(c_r2)
    c_m.append(share(feats.at[0, 2, core], mate))
    arrived(c_l2)
    c_m.append(share(feats.at[1, 2, core], mate))
    arrived(*c_y)
    if stop == 2:
        arrived(*c_m)
        return finish()
    arrived(*c_m)
    if stop == 3:
        return finish()

    w01 = wbuf[:, :, 0:80, :].reshape(1280, 128)
    folded = wbuf[:, :, 80:128, :].reshape(768, 128).astype(f32)
    low = low_lanes(768)
    first_rows = jnp.where(low, folded, 0.0).astype(bf16).reshape(16, 48, 128)
    last_rows = jnp.where(low, pltpu.roll(folded, 64, 1), 0.0).astype(bf16).reshape(16, 48, 128)
    w2 = jnp.concatenate([first_rows, last_rows[:, 0:32]], axis=1).reshape(1280, 128)
    w01 = (w01[0:640], w01[640:1280])
    w2 = (w2[0:640], w2[640:1280])

    def forward(q):
        p01 = jnp.dot(feats[0, q, 0], w01[0], preferred_element_type=f32)
        p01 += jnp.dot(feats[0, q, 1], w01[1], preferred_element_type=f32)
        p2 = jnp.dot(feats[1, q, 0], w2[0], preferred_element_type=f32)
        p2 += jnp.dot(feats[1, q, 1], w2[1], preferred_element_type=f32)
        quarter[q, 0:128] = p01
        quarter[q, 128:192] = p2[0:64] + pltpu.roll(p2[64:128], 64, 1)

    lo, hi = pl.ds(0, 96), pl.ds(96, 96)
    forward(z2)
    c_a1 = put(quarter.at[z2, lo], rs_half.at[0], above)
    c_b1 = put(quarter.at[z2, hi], rs_half.at[1], below)
    forward(zu)
    c_a2 = put(quarter.at[zu, hi], rs_full.at[0, hi], above)
    forward(zd)
    c_b2 = put(quarter.at[zd, lo], rs_full.at[1, lo], below)
    forward(zh)
    arrived(c_a1)
    quarter[zu, 0:96] += rs_half[0]
    c_a3 = put(quarter.at[zu, lo], rs_full.at[0, lo], above)
    arrived(c_b1)
    quarter[zd, 96:192] += rs_half[1]
    c_b3 = put(quarter.at[zd, hi], rs_full.at[1, hi], below)
    for n in (0, 1):
        for q in range(4):
            for d in (0, 1):
                block = feats[n, q, d].T.reshape(2, 320, 128)
                featT[n, 2 * d : 2 * d + 2, :, 128 * q : 128 * q + 128] = block
    arrived(c_a2, c_b2, c_a3, c_b3)
    if stop == 4:
        return finish()

    total = quarter[zh] + rs_full[0] + rs_full[1]
    gate = total[0:128]
    upval = pltpu.roll(gate, 64, 1)
    dhidden = jnp.concatenate([total[128:192], pltpu.roll(total[128:192], 64, 1)], axis=0)
    sigma = jax.nn.sigmoid(gate)
    hidden = gate * sigma * upval
    dgate = dhidden * upval * sigma * (1.0 + gate * (1.0 - sigma))
    dup = dhidden * gate * sigma
    low = low_lanes(128)
    dcat[zh, 0:128] = jnp.where(low, dgate, pltpu.roll(dup, 64, 1)).astype(bf16)
    hidden = jnp.where(low[0:64], hidden[0:64], pltpu.roll(hidden[64:128], 64, 1))
    dcat[zh, 128:192] = hidden.astype(bf16)

    c_a1, c_b1 = share(dcat.at[zh, lo], above), share(dcat.at[zh, hi], below)
    c_a2, c_b2 = share(dcat.at[zh, hi], above), share(dcat.at[zh, lo], below)
    arrived(c_a1)
    c_a3 = share(dcat.at[zd, lo], above)
    arrived(c_b1)
    c_b3 = share(dcat.at[zu, hi], below)
    arrived(c_a2, c_b2, c_a3, c_b3)
    if stop == 5:
        return finish()

    d01 = dcat[:, 0:128, :].reshape(512, 128)
    low = low_lanes(256)
    folded = dcat[:, 128:192, :].reshape(256, 128).astype(f32)
    early = jnp.where(low, folded, 0.0).astype(bf16).reshape(4, 64, 128)
    late = jnp.where(low, pltpu.roll(folded, 64, 1), 0.0).astype(bf16).reshape(4, 64, 128)
    d2 = jnp.concatenate([early, late], axis=1).reshape(512, 128)

    def backward(v):
        p01 = jnp.dot(featT[0, v], d01, preferred_element_type=f32)
        p2 = jnp.dot(featT[1, v], d2, preferred_element_type=f32).reshape(4, 80, 128)
        rest = pltpu.roll(p2[:, 40:80].reshape(160, 128), 64, 1).reshape(4, 40, 128)
        gbuf[v, :, 0:80] = p01.reshape(4, 80, 128)
        gbuf[v, :, 80:120] = p2[:, 0:40] + rest

    lo, hi = pl.ds(0, 2), pl.ds(2, 2)
    backward(flip(y2))
    c_a1 = put(gbuf.at[flip(y2), lo], gy_half.at[0], up)
    c_b1 = put(gbuf.at[flip(y2), hi], gy_half.at[1], down)
    backward(flip(yu))
    c_a2 = put(gbuf.at[flip(yu), hi], gy_full.at[0, hi], up)
    backward(flip(yd))
    c_b2 = put(gbuf.at[flip(yd), lo], gy_full.at[1, lo], down)
    backward(flip(y))
    arrived(c_a1)
    gbuf[flip(yu), 0:2] += gy_half[0]
    c_a3 = put(gbuf.at[flip(yu), lo], gy_full.at[0, lo], up)
    arrived(c_b1)
    gbuf[flip(yd), 2:4] += gy_half[1]
    c_b3 = put(gbuf.at[flip(yd), hi], gy_full.at[1, hi], down)
    arrived(c_a2, c_b2, c_a3, c_b3)
    gline[...] = gbuf[flip(y)] + gy_full[0] + gy_full[1]
    if stop == 6:
        return finish()
    c_z = [put(gline.at[(z + k) % 4], gz_in.at[k - 1], skew[k - 1]) for k in (1, 2, 3)]
    arrived(*c_z)
    gline[z] += gz_in[0] + gz_in[1] + gz_in[2]
    if stop == 7:
        return finish()

    arrived(put(gline.at[z], gin, owners[0]))
    if stop == 8:
        return finish()

    g01 = gin[0:80]
    g2 = jnp.concatenate([gin[80:120], pltpu.roll(gin[80:120], 64, 1)], axis=0)
    grads = jnp.concatenate([g01.T, g2.T[0:64]], axis=0).reshape(3, 64, 80)
    fresh = adamw(grads, state[0], state[1], state[2])[2]
    fin[y, x, 0] = shard_block(fresh.reshape(192, 80))

    c_z = [put(fin.at[y, x, 0], fin.at[y, x, 4 - k], line[k - 1]) for k in (1, 2, 3)]
    grads_own[...] = grads
    stores = [pltpu.make_async_copy(grads_own, grads_out, store_sems.at[0])]
    stores[0].start()

    class Plane:
        def __init__(self, slots):
            self.slots = slots

        def at(self, yy, xx, start=0, size=128):
            return fin.at[yy, xx, self.slots, pl.ds(start, size)]

        def begin(self):
            mine = self.at(y, x)
            self.r, self.l, self.u, self.d = (share(mine, to) for to in (right, left, up, down))
            self.x2 = share(self.at(y, x, 0, 64), across_x)
            self.y2 = share(self.at(y, x, 64, 64), across_y)

        def turn(self):
            def columns(xx):
                return [share(self.at(y, xx, 0, 64), to) for to in (up, down)]

            def rows(yy):
                return [share(self.at(yy, x, 64, 64), to) for to in (right, left)]

            arrived(self.r)
            self.a = [columns(xd)]
            self.last = [share(self.at(y, xd, 64, 32), right)]
            arrived(self.u)
            self.b = [rows(yd)]
            self.last.append(share(self.at(yd, x, 0, 32), up))
            arrived(self.l)
            self.a.append(columns(xu))
            self.last.append(share(self.at(y, xu, 96, 32), left))
            arrived(self.d)
            self.b.append(rows(yu))
            self.last.append(share(self.at(yu, x, 32, 32), down))
            arrived(self.x2)
            self.a.append(columns(x2))
            arrived(self.y2)
            self.b.append(rows(y2))

        def forward(self):
            for xx, yy, a, b in zip((xd, xu, x2), (yd, yu, y2), self.a, self.b):
                arrived(a[0])
                self.last.append(share(self.at(yd, xx, 0, 32), up))
                arrived(b[0])
                self.last.append(share(self.at(yy, xd, 64, 32), right))
                arrived(a[1])
                self.last.append(share(self.at(yu, xx, 32, 32), down))
                arrived(b[1])
                self.last.append(share(self.at(yy, xu, 96, 32), left))

        def end(self):
            arrived(*self.last)

    def unpack(r):
        n = (z + r) % 4
        both = fin[:, :, r, 0:80, :].reshape(1280, 128).T
        rows_new[n, 0] = both[0:64]
        rows_new[n, 1] = both[64:128]
        folded = fin[:, :, r, 80:128, :].reshape(768, 128).astype(f32)
        rest = pltpu.roll(folded, 64, 1).reshape(16, 48, 128)[:, 0:32]
        third = jnp.concatenate([folded.reshape(16, 48, 128), rest], axis=1)
        rows_new[n, 2] = third.reshape(1280, 128).astype(bf16).T[0:64]
        columns = pl.ds(pl.multiple_of(n * 1280, 128), 1280)
        store = pltpu.make_async_copy(
            rows_new.at[n], weights_out.at[:, :, columns], store_sems.at[1 + r]
        )
        store.start()
        stores.append(store)

    near, far = Plane(pl.ds(0, 1)), Plane(pl.ds(1, 3))
    near.begin()
    near.turn()
    arrived(*c_z)
    if stop == 9:
        near.forward()
        near.end()
        stores[0].wait()
        return finish()
    far.begin()
    near.forward()
    far.turn()
    near.end()
    unpack(0)
    far.forward()
    far.end()
    if stop == 10:
        for store in stores:
            store.wait()
        return finish()
    for r in (1, 2, 3):
        unpack(r)
    for store in stores:
        store.wait()
    finish()


def local(stop, inputs, upstream, master, moment_one, moment_two):
    shard = jax.ShapeDtypeStruct((3, 64, 80), f32)
    hbm = pl.BlockSpec(memory_space=pltpu.HBM)
    grads, weights = pl.pallas_call(
        functools.partial(kernel, stop),
        out_shape=(shard, jax.ShapeDtypeStruct((3, 64, 5120), bf16)),
        in_specs=[hbm] * 5,
        out_specs=(hbm,) * 2,
        scratch_shapes=[
            pltpu.VMEM((2, 4, 2, 128, 640), bf16),
            pltpu.VMEM((3, 3, 64, 80), f32),
            pltpu.VMEM((3, 64, 80), f32),
            pltpu.VMEM((128, 128), bf16),
            pltpu.VMEM((4, 4, 128, 128), bf16),
            pltpu.VMEM((4, 192, 128), f32),
            pltpu.VMEM((2, 96, 128), f32),
            pltpu.VMEM((2, 192, 128), f32),
            pltpu.VMEM((4, 192, 128), bf16),
            pltpu.VMEM((2, 4, 320, 512), bf16),
            pltpu.VMEM((4, 4, 120, 128), f32),
            pltpu.VMEM((2, 2, 120, 128), f32),
            pltpu.VMEM((2, 4, 120, 128), f32),
            pltpu.VMEM((4, 120, 128), f32),
            pltpu.VMEM((3, 120, 128), f32),
            pltpu.VMEM((120, 128), f32),
            pltpu.VMEM((4, 4, 4, 128, 128), bf16),
            pltpu.VMEM((4, 3, 64, 1280), bf16),
            pltpu.SemaphoreType.DMA((N_COPIES,)),
            pltpu.SemaphoreType.DMA((N_COPIES,)),
            pltpu.SemaphoreType.DMA((5,)),
            pltpu.SemaphoreType.DMA((5,)),
        ],
        compiler_params=pltpu.CompilerParams(
            collective_id=0, has_side_effects=True, vmem_limit_bytes=62 * 2**20
        ),
        cost_estimate=pl.CostEstimate(
            flops=503316480, bytes_accessed=8000000, transcendentals=8192
        ),
        name="fused_step",
    )(inputs, upstream, master, moment_one, moment_two)
    first, second, fresh = adamw(grads, master, moment_one, moment_two)
    return fresh, first, second, weights


def solution(mesh, stop=0):
    owned = P(None, "mp", "dp")
    return jax.shard_map(
        functools.partial(local, stop),
        mesh=mesh,
        in_specs=(P("dp", "mp"), P("dp", "mp"), owned, owned, owned),
        out_specs=(owned, owned, owned, P(None, "mp", None)),
        check_vma=False,
    )
```

```python
import functools

import jax
import jax.numpy as jnp
from jax import lax
from jax.experimental import pallas as pl
from jax.experimental.pallas import tpu as pltpu
from jax.sharding import PartitionSpec as P

beta_one = 0.9
beta_two = 0.95
learn_rate = 0.0003
decay_rate = 0.1
eps_small = 1e-08
corr_one = 1.0 - 0.9**40
corr_two = 1.0 - 0.95**40

MESH = pl.DeviceIdType.MESH
f32 = jnp.float32
bf16 = jnp.bfloat16
N_COPIES = 160


def adamw(grads, master, moment_one, moment_two):
    first = beta_one * moment_one + (1.0 - beta_one) * grads
    second = beta_two * moment_two + (1.0 - beta_two) * grads * grads
    update = first / corr_one / (jnp.sqrt(second / corr_two) + eps_small)
    return first, second, master - learn_rate * (update + decay_rate * master)


def kernel(
    stop,
    inputs_hbm, upstream_hbm, master_hbm, moment_one_hbm, moment_two_hbm,
    grads_out, weights_out,
    feats, state, grads_own, wown, wbuf, quarter, rs_half, rs_full, dcat,
    featT, gbuf, gy_half, gy_full, gline, gz_in, gin, fin, rows_new,
    send_sems, recv_sems, load_sems, store_sems,
):
    i, j = lax.axis_index("dp"), lax.axis_index("mp")
    z, y, x = i // 16, (i // 4) % 4, i % 4
    zh, core = j // 2, j % 2

    def dev(zh=zh, core=core, z=z, y=y, x=x):
        return (z * 16 + y * 4 + x, zh * 2 + core)

    flip = lambda v: v + 1 - 2 * (v % 2)
    xu, xd, x2 = (x + 1) % 4, (x + 3) % 4, (x + 2) % 4
    yu, yd, y2 = (y + 1) % 4, (y + 3) % 4, (y + 2) % 4
    zu, zd, z2 = (zh + 1) % 4, (zh + 3) % 4, (zh + 2) % 4
    right, left, up, down = dev(x=xu), dev(x=xd), dev(y=yu), dev(y=yd)
    across_x, across_y = dev(x=x2), dev(y=y2)
    line = [dev(z=(z + k) % 4) for k in (1, 2, 3)]
    skew = [dev(z=(z + k) % 4, x=(x + k) % 4) for k in (1, 2, 3)]
    above, below = dev(zh=zu), dev(zh=zd)
    opposed, mate = dev(zh=z2), dev(core=1 - core)
    holders = [
        dev(zh=z, z=(x + m) % 4, y=flip(y), x=(zh + x + m) % 4) for m in range(4)
    ]
    owners = [
        dev(zh=(x + 4 - z) % 4, z=zh, y=flip(y), x=(z + 4 - m) % 4) for m in range(4)
    ]

    started = []

    def put(src, dst, to):
        k = len(started)
        copy = pltpu.make_async_remote_copy(
            src_ref=src, dst_ref=dst, send_sem=send_sems.at[k], recv_sem=recv_sems.at[k],
            device_id=to, device_id_type=MESH,
        )
        copy.start()
        started.append(copy)
        return copy

    def share(ref, to):
        return put(ref, ref, to)

    def arrived(*copies):
        for copy in copies:
            copy.wait_recv()

    def finish():
        for copy in started:
            copy.wait_send()

    barrier = pltpu.get_barrier_semaphore()
    greeted = [
        *holders, *owners, above, below, opposed, *line, *skew,
        right, left, up, down, across_x, across_y, mate,
    ]
    for other in greeted:
        pl.semaphore_signal(barrier, inc=1, device_id=other, device_id_type=MESH)

    loads = [
        pltpu.make_async_copy(src, dst, load_sems.at[k])
        for k, (src, dst) in enumerate([
            (master_hbm, state.at[0]),
            (inputs_hbm, feats.at[0, 0, core]),
            (upstream_hbm, feats.at[1, 0, core]),
            (moment_one_hbm, state.at[1]),
            (moment_two_hbm, state.at[2]),
        ])
    ]
    for load in loads:
        load.start()

    def low_lanes(n):
        return lax.broadcasted_iota(jnp.int32, (n, 128), 1) < 64

    def shard_block(rows):
        down_cols = jnp.concatenate([rows[128:192], jnp.zeros((64, 80), f32)], axis=0).T
        rest = jnp.concatenate([down_cols[48:80], jnp.zeros((16, 128), f32)], axis=0)
        folded = down_cols[0:48] + pltpu.roll(rest, 64, 1)
        return jnp.concatenate([rows[0:128].T, folded], axis=0).astype(bf16)

    loads[0].wait()
    wown[...] = shard_block(state[0].reshape(192, 80))
    for load in loads[1:]:
        load.wait()

    pl.semaphore_wait(barrier, len(greeted))

    gate_up, down_part = pl.ds(0, 80), pl.ds(80, 48)
    c_w = [
        [put(wown.at[rows], wbuf.at[y, x, rows], to) for to in holders]
        for rows in (gate_up, down_part)
    ]
    own = [feats.at[n, 0, core] for n in (0, 1)]
    c_r, c_l = [], []
    for n in (0, 1):
        c_r.append(put(own[n], feats.at[n, 3, core], right))
        c_l.append(put(own[n], feats.at[n, 1, core], left))
    c_m = [[share(own[n], mate)] for n in (0, 1)]
    c_y = [[], []]

    def spread(n, m):
        arrived(c_w[n][m])
        piece = wbuf.at[flip(y), (z + 4 - m) % 4, (gate_up, down_part)[n]]
        c_y[n].extend(share(piece, to) for to in (up, down, across_y))

    spread(0, 0)
    spread(0, 1)
    arrived(c_r[0])
    c_r2 = put(feats.at[0, 3, core], feats.at[0, 2, core], right)
    c_m[0].append(share(feats.at[0, 3, core], mate))
    spread(0, 2)
    spread(0, 3)
    arrived(c_l[0])
    c_m[0].append(share(feats.at[0, 1, core], mate))
    arrived(c_l[1])
    c_l2 = put(feats.at[1, 1, core], feats.at[1, 2, core], left)
    c_m[1].append(share(feats.at[1, 1, core], mate))
    for m in range(4):
        spread(1, m)
    arrived(c_r[1])
    c_m[1].append(share(feats.at[1, 3, core], mate))
    arrived(c_r2)
    c_m[0].append(share(feats.at[0, 2, core], mate))
    arrived(c_l2)
    c_m[1].append(share(feats.at[1, 2, core], mate))
    arrived(*c_m[0], *c_y[0])
    if stop == 1:
        arrived(*c_m[1], *c_y[1])
        return finish()

    w01 = wbuf[:, :, 0:80, :].reshape(1280, 128)
    w01 = (w01[0:640], w01[640:1280])

    def forward01(q):
        p01 = jnp.dot(feats[0, q, 0], w01[0], preferred_element_type=f32)
        p01 += jnp.dot(feats[0, q, 1], w01[1], preferred_element_type=f32)
        quarter[q, 0:128] = p01

    def forward2(q):
        p2 = jnp.dot(feats[1, q, 0], w2[0], preferred_element_type=f32)
        p2 += jnp.dot(feats[1, q, 1], w2[1], preferred_element_type=f32)
        quarter[q, 128:192] = p2[0:64] + pltpu.roll(p2[64:128], 64, 1)

    lo, hi = (pl.ds(0, 64), pl.ds(128, 32)), (pl.ds(64, 64), pl.ds(160, 32))

    def opposite(n):
        return (
            put(quarter.at[z2, lo[n]], rs_half.at[lo[n]], above),
            put(quarter.at[z2, hi[n]], rs_half.at[hi[n]], below),
        )

    def direct(n):
        return (
            put(quarter.at[zu, hi[n]], rs_full.at[0, hi[n]], above),
            put(quarter.at[zd, lo[n]], rs_full.at[1, lo[n]], below),
        )

    def onward(n, c_a, c_b):
        arrived(c_a)
        quarter[zu, lo[n]] += rs_half[lo[n]]
        c_up = put(quarter.at[zu, lo[n]], rs_full.at[0, lo[n]], above)
        arrived(c_b)
        quarter[zd, hi[n]] += rs_half[hi[n]]
        return c_up, put(quarter.at[zd, hi[n]], rs_full.at[1, hi[n]], below)

    forward01(z2)
    c_o1 = opposite(0)
    forward01(zu)
    forward01(zd)
    arrived(*c_m[1], *c_y[1])
    folded = wbuf[:, :, 80:128, :].reshape(768, 128).astype(f32)
    low = low_lanes(768)
    first_rows = jnp.where(low, folded, 0.0).astype(bf16).reshape(16, 48, 128)
    last_rows = jnp.where(low, pltpu.roll(folded, 64, 1), 0.0).astype(bf16).reshape(16, 48, 128)
    w2 = jnp.concatenate([first_rows, last_rows[:, 0:32]], axis=1).reshape(1280, 128)
    w2 = (w2[0:640], w2[640:1280])
    forward2(z2)
    c_o2 = opposite(1)
    c_d = [*direct(0)]
    forward2(zu)
    forward2(zd)
    c_d += direct(1)
    forward01(zh)
    forward2(zh)
    c_d += onward(0, *c_o1)
    c_d += onward(1, *c_o2)
    for n in (0, 1):
        for q in range(4):
            for d in (0, 1):
                block = feats[n, q, d].T.reshape(2, 320, 128)
                featT[n, 2 * d : 2 * d + 2, :, 128 * q : 128 * q + 128] = block
    arrived(*c_d)
    if stop == 4:
        return finish()

    total = quarter[zh] + rs_full[0] + rs_full[1]
    gate = total[0:128]
    upval = pltpu.roll(gate, 64, 1)
    dhidden = jnp.concatenate([total[128:192], pltpu.roll(total[128:192], 64, 1)], axis=0)
    sigma = jax.nn.sigmoid(gate)
    hidden = gate * sigma * upval
    dgate = dhidden * upval * sigma * (1.0 + gate * (1.0 - sigma))
    dup = dhidden * gate * sigma
    low = low_lanes(128)
    dcat[zh, 0:128] = jnp.where(low, dgate, pltpu.roll(dup, 64, 1)).astype(bf16)
    hidden = jnp.where(low[0:64], hidden[0:64], pltpu.roll(hidden[64:128], 64, 1))
    dcat[zh, 128:192] = hidden.astype(bf16)

    mine = dcat.at[zh]
    c_a = [share(mine, to) for to in (opposed, above, below)]
    arrived(*c_a)
    if stop == 5:
        return finish()

    d01 = dcat[:, 0:128, :].reshape(512, 128)
    low = low_lanes(256)
    folded = dcat[:, 128:192, :].reshape(256, 128).astype(f32)
    early = jnp.where(low, folded, 0.0).astype(bf16).reshape(4, 64, 128)
    late = jnp.where(low, pltpu.roll(folded, 64, 1), 0.0).astype(bf16).reshape(4, 64, 128)
    d2 = jnp.concatenate([early, late], axis=1).reshape(512, 128)

    def backward(v):
        p01 = jnp.dot(featT[0, v], d01, preferred_element_type=f32)
        p2 = jnp.dot(featT[1, v], d2, preferred_element_type=f32).reshape(4, 80, 128)
        rest = pltpu.roll(p2[:, 40:80].reshape(160, 128), 64, 1).reshape(4, 40, 128)
        p01, p2 = p01.reshape(4, 80, 128), p2[:, 0:40] + rest
        for n in range(4):
            k = (n + 4 - z) % 4
            gbuf[v, k, 0:80] = p01[n]
            gbuf[v, k, 80:120] = p2[n]

    lo, hi = pl.ds(0, 2), pl.ds(2, 2)
    backward(flip(y2))
    c_o = [
        put(gbuf.at[flip(y2), k], gy_half.at[k], up if k < 2 else down) for k in range(4)
    ]
    backward(flip(yu))
    c_d = [put(gbuf.at[flip(yu), hi], gy_full.at[0, hi], up)]
    backward(flip(yd))
    c_d.append(put(gbuf.at[flip(yd), lo], gy_full.at[1, lo], down))
    backward(flip(y))
    c_f = [None] * 4
    for k in (1, 2, 3, 0):
        arrived(c_o[k])
        v = flip(yu) if k < 2 else flip(yd)
        gbuf[v, k] += gy_half[k]
        c_f[k] = put(gbuf.at[v, k], gy_full.at[k // 2, k], up if k < 2 else down)
    arrived(*c_d)
    c_z = []
    for k in (1, 2, 3, 0):
        arrived(c_f[k])
        gline[k] = gbuf[flip(y), k] + gy_full[0, k] + gy_full[1, k]
        if k > 0:
            c_z.append(put(gline.at[k], gz_in.at[k - 1], skew[k - 1]))
    if stop == 6:
        arrived(*c_z)
        return finish()
    arrived(*c_z)
    gline[0] += gz_in[0] + gz_in[1] + gz_in[2]
    if stop == 7:
        return finish()

    arrived(put(gline.at[0], gin, owners[0]))
    if stop == 8:
        return finish()

    g01 = gin[0:80]
    g2 = jnp.concatenate([gin[80:120], pltpu.roll(gin[80:120], 64, 1)], axis=0)
    grads = jnp.concatenate([g01.T, g2.T[0:64]], axis=0).reshape(3, 64, 80)
    fresh = adamw(grads, state[0], state[1], state[2])[2]
    fin[y, x, 0] = shard_block(fresh.reshape(192, 80))

    c_z = [put(fin.at[y, x, 0], fin.at[y, x, 4 - k], line[k - 1]) for k in (1, 2, 3)]
    grads_own[...] = grads
    stores = [pltpu.make_async_copy(grads_own, grads_out, store_sems.at[0])]
    stores[0].start()

    class Plane:
        def __init__(self, slots):
            self.slots = slots

        def at(self, yy, xx, start=0, size=128):
            return fin.at[yy, xx, self.slots, pl.ds(start, size)]

        def begin(self):
            a, b = self.at(y, x, 0, 64), self.at(y, x, 64, 64)
            self.ax = [share(a, to) for to in (right, left, across_x)]
            self.by = [share(b, to) for to in (up, down, across_y)]
            self.own = [share(a, up), share(b, right), share(a, down), share(b, left)]

        def turn(self):
            self.a, self.b = [], []
            for n, (xx, yy) in enumerate(((xd, yd), (xu, yu), (x2, y2))):
                arrived(self.ax[n])
                self.a.append([share(self.at(y, xx, 0, 64), to) for to in (up, down)])
                arrived(self.by[n])
                self.b.append([share(self.at(yy, x, 64, 64), to) for to in (right, left)])

        def forward(self):
            self.last = []
            au, br, ad, bl = self.own
            pairs = [(x, y, (au, ad), (br, bl))]
            pairs += zip((xd, xu, x2), (yd, yu, y2), self.a, self.b)
            for xx, yy, a, b in pairs:
                arrived(a[0])
                self.last.append(share(self.at(yd, xx, 0, 32), up))
                arrived(b[0])
                self.last.append(share(self.at(yy, xd, 64, 32), right))
                arrived(a[1])
                self.last.append(share(self.at(yu, xx, 32, 32), down))
                arrived(b[1])
                self.last.append(share(self.at(yy, xu, 96, 32), left))

        def end(self):
            arrived(*self.last)

    def unpack(r):
        n = (z + r) % 4
        both = fin[:, :, r, 0:80, :].reshape(1280, 128).T
        rows_new[n, 0] = both[0:64]
        rows_new[n, 1] = both[64:128]
        folded = fin[:, :, r, 80:128, :].reshape(768, 128).astype(f32)
        rest = pltpu.roll(folded, 64, 1).reshape(16, 48, 128)[:, 0:32]
        third = jnp.concatenate([folded.reshape(16, 48, 128), rest], axis=1)
        rows_new[n, 2] = third.reshape(1280, 128).astype(bf16).T[0:64]
        columns = pl.ds(pl.multiple_of(n * 1280, 128), 1280)
        store = pltpu.make_async_copy(
            rows_new.at[n], weights_out.at[:, :, columns], store_sems.at[1 + r]
        )
        store.start()
        stores.append(store)

    near, far = Plane(pl.ds(0, 1)), Plane(pl.ds(1, 3))
    near.begin()
    near.turn()
    arrived(*c_z)
    if stop == 9:
        near.forward()
        near.end()
        stores[0].wait()
        return finish()
    far.begin()
    near.forward()
    far.turn()
    near.end()
    unpack(0)
    far.forward()
    far.end()
    if stop == 10:
        for store in stores:
            store.wait()
        return finish()
    for r in (1, 2, 3):
        unpack(r)
    for store in stores:
        store.wait()
    finish()


def local(stop, inputs, upstream, master, moment_one, moment_two):
    shard = jax.ShapeDtypeStruct((3, 64, 80), f32)
    hbm = pl.BlockSpec(memory_space=pltpu.HBM)
    grads, weights = pl.pallas_call(
        functools.partial(kernel, stop),
        out_shape=(shard, jax.ShapeDtypeStruct((3, 64, 5120), bf16)),
        in_specs=[hbm] * 5,
        out_specs=(hbm,) * 2,
        scratch_shapes=[
            pltpu.VMEM((2, 4, 2, 128, 640), bf16),
            pltpu.VMEM((3, 3, 64, 80), f32),
            pltpu.VMEM((3, 64, 80), f32),
            pltpu.VMEM((128, 128), bf16),
            pltpu.VMEM((4, 4, 128, 128), bf16),
            pltpu.VMEM((4, 192, 128), f32),
            pltpu.VMEM((192, 128), f32),
            pltpu.VMEM((2, 192, 128), f32),
            pltpu.VMEM((4, 192, 128), bf16),
            pltpu.VMEM((2, 4, 320, 512), bf16),
            pltpu.VMEM((4, 4, 120, 128), f32),
            pltpu.VMEM((4, 120, 128), f32),
            pltpu.VMEM((2, 4, 120, 128), f32),
            pltpu.VMEM((4, 120, 128), f32),
            pltpu.VMEM((3, 120, 128), f32),
            pltpu.VMEM((120, 128), f32),
            pltpu.VMEM((4, 4, 4, 128, 128), bf16),
            pltpu.VMEM((4, 3, 64, 1280), bf16),
            pltpu.SemaphoreType.DMA((N_COPIES,)),
            pltpu.SemaphoreType.DMA((N_COPIES,)),
            pltpu.SemaphoreType.DMA((5,)),
            pltpu.SemaphoreType.DMA((5,)),
        ],
        compiler_params=pltpu.CompilerParams(
            collective_id=0, has_side_effects=True, vmem_limit_bytes=62 * 2**20
        ),
        cost_estimate=pl.CostEstimate(
            flops=503316480, bytes_accessed=8000000, transcendentals=8192
        ),
        name="fused_step",
    )(inputs, upstream, master, moment_one, moment_two)
    first, second, fresh = adamw(grads, master, moment_one, moment_two)
    return fresh, first, second, weights


def solution(mesh, stop=0):
    owned = P(None, "mp", "dp")
    return jax.shard_map(
        functools.partial(local, stop),
        mesh=mesh,
        in_specs=(P("dp", "mp"), P("dp", "mp"), owned, owned, owned),
        out_specs=(owned, owned, owned, P(None, "mp", None)),
        check_vma=False,
    )
```

```python
import functools

import jax
import jax.numpy as jnp
from jax import lax
from jax.experimental import pallas as pl
from jax.experimental.pallas import tpu as pltpu
from jax.sharding import PartitionSpec as P

beta_one = 0.9
beta_two = 0.95
learn_rate = 0.0003
decay_rate = 0.1
eps_small = 1e-08
corr_one = 1.0 - 0.9**40
corr_two = 1.0 - 0.95**40

MESH = pl.DeviceIdType.MESH
f32 = jnp.float32
bf16 = jnp.bfloat16
N_COPIES = 208


def adamw(grads, master, moment_one, moment_two):
    first = beta_one * moment_one + (1.0 - beta_one) * grads
    second = beta_two * moment_two + (1.0 - beta_two) * grads * grads
    update = first / corr_one / (jnp.sqrt(second / corr_two) + eps_small)
    return first, second, master - learn_rate * (update + decay_rate * master)


def kernel(
    stop,
    inputs_hbm, upstream_hbm, master_hbm, moment_one_hbm, moment_two_hbm,
    grads_out, weights_out,
    feats, state, wown, wbuf, quarter, rs_half, rs_full, dcat,
    featT, gbuf, gy_half, gy_full, gline, gz_in, gin, fin,
    send_sems, recv_sems, load_sems,
):
    i, j = lax.axis_index("dp"), lax.axis_index("mp")
    z, y, x = i // 16, (i // 4) % 4, i % 4
    zh, core = j // 2, j % 2

    def dev(zh=zh, core=core, z=z, y=y, x=x):
        return (z * 16 + y * 4 + x, zh * 2 + core)

    flip = lambda v: v + 1 - 2 * (v % 2)
    xu, xd, x2 = (x + 1) % 4, (x + 3) % 4, (x + 2) % 4
    yu, yd, y2 = (y + 1) % 4, (y + 3) % 4, (y + 2) % 4
    zu, zd, z2 = (zh + 1) % 4, (zh + 3) % 4, (zh + 2) % 4
    right, left, up, down = dev(x=xu), dev(x=xd), dev(y=yu), dev(y=yd)
    across_x, across_y = dev(x=x2), dev(y=y2)
    line = [dev(z=(z + k) % 4) for k in (1, 2, 3)]
    skew = [dev(z=(z + k) % 4, x=(x + k) % 4) for k in (1, 2, 3)]
    above, below = dev(zh=zu), dev(zh=zd)
    mate = dev(core=1 - core)
    holders = [
        dev(zh=z, z=(x + m) % 4, y=flip(y), x=(zh + x + m) % 4) for m in range(4)
    ]
    owners = [
        dev(zh=(x + 4 - z) % 4, z=zh, y=flip(y), x=(z + 4 - m) % 4) for m in range(4)
    ]

    started = []

    def put(src, dst, to):
        k = len(started)
        copy = pltpu.make_async_remote_copy(
            src_ref=src, dst_ref=dst, send_sem=send_sems.at[k], recv_sem=recv_sems.at[k],
            device_id=to, device_id_type=MESH,
        )
        copy.start()
        started.append(copy)
        return copy

    def share(ref, to):
        return put(ref, ref, to)

    def arrived(*copies):
        for copy in copies:
            copy.wait_recv()

    def finish():
        for copy in started:
            copy.wait_send()

    barrier = pltpu.get_barrier_semaphore()
    greeted = [
        *holders, *owners, above, below, *line, *skew,
        right, left, up, down, across_x, across_y, mate,
    ]
    for other in greeted:
        pl.semaphore_signal(barrier, inc=1, device_id=other, device_id_type=MESH)

    loads = [
        pltpu.make_async_copy(src, dst, load_sems.at[k])
        for k, (src, dst) in enumerate([
            (master_hbm, state.at[0]),
            (inputs_hbm, feats.at[0, 0, core]),
            (upstream_hbm, feats.at[1, 0, core]),
            (moment_one_hbm, state.at[1]),
            (moment_two_hbm, state.at[2]),
        ])
    ]
    for load in loads:
        load.start()

    def low_lanes(n):
        return lax.broadcasted_iota(jnp.int32, (n, 128), 1) < 64

    def shard_block(rows):
        down_cols = jnp.concatenate([rows[128:192], jnp.zeros((64, 80), f32)], axis=0).T
        rest = jnp.concatenate([down_cols[48:80], jnp.zeros((16, 128), f32)], axis=0)
        folded = down_cols[0:48] + pltpu.roll(rest, 64, 1)
        return jnp.concatenate([rows[0:128].T, folded], axis=0).astype(bf16)

    loads[0].wait()
    wown[...] = shard_block(state[0].reshape(192, 80))
    for load in loads[1:]:
        load.wait()

    pl.semaphore_wait(barrier, len(greeted))

    gate_up, down_part = pl.ds(0, 80), pl.ds(80, 48)
    c_w = [
        [put(wown.at[rows], wbuf.at[y, x, rows], to) for to in holders]
        for rows in (gate_up, down_part)
    ]
    own = [feats.at[n, 0, core] for n in (0, 1)]
    c_r, c_l = [], []
    for n in (0, 1):
        c_r.append(put(own[n], feats.at[n, 3, core], right))
        c_l.append(put(own[n], feats.at[n, 1, core], left))
    c_m = [[share(own[n], mate)] for n in (0, 1)]
    c_y = [[], []]

    def spread(n, m):
        arrived(c_w[n][m])
        piece = wbuf.at[flip(y), (z + 4 - m) % 4, (gate_up, down_part)[n]]
        c_y[n].extend(share(piece, to) for to in (up, down, across_y))

    spread(0, 0)
    spread(0, 1)
    arrived(c_r[0])
    c_r2 = put(feats.at[0, 3, core], feats.at[0, 2, core], right)
    c_m[0].append(share(feats.at[0, 3, core], mate))
    spread(0, 2)
    spread(0, 3)
    arrived(c_l[0])
    c_m[0].append(share(feats.at[0, 1, core], mate))
    arrived(c_l[1])
    c_l2 = put(feats.at[1, 1, core], feats.at[1, 2, core], left)
    c_m[1].append(share(feats.at[1, 1, core], mate))
    for m in range(4):
        spread(1, m)
    arrived(c_r[1])
    c_m[1].append(share(feats.at[1, 3, core], mate))
    arrived(c_r2)
    c_m[0].append(share(feats.at[0, 2, core], mate))
    arrived(c_l2)
    c_m[1].append(share(feats.at[1, 2, core], mate))
    arrived(*c_m[0], *c_y[0])
    if stop == 1:
        arrived(*c_m[1], *c_y[1])
        return finish()

    w01 = wbuf[:, :, 0:80, :].reshape(1280, 128)
    w01 = (w01[0:640], w01[640:1280])

    def forward01(q):
        p01 = jnp.dot(feats[0, q, 0], w01[0], preferred_element_type=f32)
        p01 += jnp.dot(feats[0, q, 1], w01[1], preferred_element_type=f32)
        quarter[q, 0:128] = p01

    def forward2(q):
        p2 = jnp.dot(feats[1, q, 0], w2[0], preferred_element_type=f32)
        p2 += jnp.dot(feats[1, q, 1], w2[1], preferred_element_type=f32)
        quarter[q, 128:192] = p2[0:64] + pltpu.roll(p2[64:128], 64, 1)

    lo, hi = (pl.ds(0, 64), pl.ds(128, 32)), (pl.ds(64, 64), pl.ds(160, 32))

    def opposite(n):
        return (
            put(quarter.at[z2, lo[n]], rs_half.at[lo[n]], above),
            put(quarter.at[z2, hi[n]], rs_half.at[hi[n]], below),
        )

    def direct(n):
        return (
            put(quarter.at[zu, hi[n]], rs_full.at[0, hi[n]], above),
            put(quarter.at[zd, lo[n]], rs_full.at[1, lo[n]], below),
        )

    def onward(n, c_a, c_b):
        arrived(c_a)
        quarter[zu, lo[n]] += rs_half[lo[n]]
        c_up = put(quarter.at[zu, lo[n]], rs_full.at[0, lo[n]], above)
        arrived(c_b)
        quarter[zd, hi[n]] += rs_half[hi[n]]
        return c_up, put(quarter.at[zd, hi[n]], rs_full.at[1, hi[n]], below)

    forward01(z2)
    c_o1 = opposite(0)
    forward01(zu)
    forward01(zd)
    arrived(*c_m[1], *c_y[1])
    folded = wbuf[:, :, 80:128, :].reshape(768, 128).astype(f32)
    low = low_lanes(768)
    first_rows = jnp.where(low, folded, 0.0).astype(bf16).reshape(16, 48, 128)
    last_rows = jnp.where(low, pltpu.roll(folded, 64, 1), 0.0).astype(bf16).reshape(16, 48, 128)
    w2 = jnp.concatenate([first_rows, last_rows[:, 0:32]], axis=1).reshape(1280, 128)
    w2 = (w2[0:640], w2[640:1280])
    forward2(z2)
    c_o2 = opposite(1)
    c_d = [*direct(0)]
    forward2(zu)
    forward2(zd)
    c_d += direct(1)
    forward01(zh)
    forward2(zh)
    c_d += onward(0, *c_o1)
    c_d += onward(1, *c_o2)
    for n in (0, 1):
        for q in range(4):
            for d in (0, 1):
                block = feats[n, q, d].T.reshape(2, 320, 128)
                featT[n, 2 * d : 2 * d + 2, :, 128 * q : 128 * q + 128] = block
    arrived(*c_d)
    if stop == 4:
        return finish()

    total = quarter[zh] + rs_full[0] + rs_full[1]
    gate = total[0:128]
    upval = pltpu.roll(gate, 64, 1)
    dhidden = jnp.concatenate([total[128:192], pltpu.roll(total[128:192], 64, 1)], axis=0)
    sigma = jax.nn.sigmoid(gate)
    hidden = gate * sigma * upval
    dgate = dhidden * upval * sigma * (1.0 + gate * (1.0 - sigma))
    dup = dhidden * gate * sigma
    low = low_lanes(128)
    dcat[zh, 0:128] = jnp.where(low, dgate, pltpu.roll(dup, 64, 1)).astype(bf16)
    hidden = jnp.where(low[0:64], hidden[0:64], pltpu.roll(hidden[64:128], 64, 1))
    dcat[zh, 128:192] = hidden.astype(bf16)

    lo, hi = pl.ds(0, 96), pl.ds(96, 96)
    c_a1, c_b1 = share(dcat.at[zh, lo], above), share(dcat.at[zh, hi], below)
    c_a2, c_b2 = share(dcat.at[zh, hi], above), share(dcat.at[zh, lo], below)
    arrived(c_a1)
    c_a3 = share(dcat.at[zd, lo], above)
    arrived(c_b1)
    c_b3 = share(dcat.at[zu, hi], below)
    arrived(c_a2, c_b2, c_a3, c_b3)
    if stop == 5:
        return finish()

    d01 = dcat[:, 0:128, :].reshape(512, 128)
    low = low_lanes(256)
    folded = dcat[:, 128:192, :].reshape(256, 128).astype(f32)
    early = jnp.where(low, folded, 0.0).astype(bf16).reshape(4, 64, 128)
    late = jnp.where(low, pltpu.roll(folded, 64, 1), 0.0).astype(bf16).reshape(4, 64, 128)
    d2 = jnp.concatenate([early, late], axis=1).reshape(512, 128)

    def backward(v):
        p01 = jnp.dot(featT[0, v], d01, preferred_element_type=f32)
        p2 = jnp.dot(featT[1, v], d2, preferred_element_type=f32).reshape(4, 80, 128)
        rest = pltpu.roll(p2[:, 40:80].reshape(160, 128), 64, 1).reshape(4, 40, 128)
        p01, p2 = p01.reshape(4, 80, 128), p2[:, 0:40] + rest
        for n in range(4):
            k = (n + 4 - z) % 4
            gbuf[v, k, 0:80] = p01[n]
            gbuf[v, k, 80:120] = p2[n]

    lo, hi = pl.ds(0, 2), pl.ds(2, 2)
    backward(flip(y2))
    c_o = [
        put(gbuf.at[flip(y2), k], gy_half.at[k], up if k < 2 else down) for k in range(4)
    ]
    backward(flip(yu))
    c_d = [put(gbuf.at[flip(yu), hi], gy_full.at[0, hi], up)]
    backward(flip(yd))
    c_d.append(put(gbuf.at[flip(yd), lo], gy_full.at[1, lo], down))
    backward(flip(y))
    c_f = [None] * 4
    for k in (1, 2, 3, 0):
        arrived(c_o[k])
        v = flip(yu) if k < 2 else flip(yd)
        gbuf[v, k] += gy_half[k]
        c_f[k] = put(gbuf.at[v, k], gy_full.at[k // 2, k], up if k < 2 else down)
    arrived(*c_d)
    c_z = []
    for k in (1, 2, 3, 0):
        arrived(c_f[k])
        gline[k] = gbuf[flip(y), k] + gy_full[0, k] + gy_full[1, k]
        if k > 0:
            c_z.append(put(gline.at[k], gz_in.at[k - 1], skew[k - 1]))
    if stop == 6:
        arrived(*c_z)
        return finish()
    arrived(*c_z)
    gline[0] += gz_in[0] + gz_in[1] + gz_in[2]
    if stop == 7:
        return finish()

    arrived(put(gline.at[0], gin, owners[0]))
    if stop == 8:
        return finish()

    g01 = gin[0:80]
    g2 = jnp.concatenate([gin[80:120], pltpu.roll(gin[80:120], 64, 1)], axis=0)
    grads = jnp.concatenate([g01.T, g2.T[0:64]], axis=0).reshape(3, 64, 80)
    fresh = adamw(grads, state[0], state[1], state[2])[2]
    fin[y, x, 0] = shard_block(fresh.reshape(192, 80))

    c_z = [put(fin.at[y, x, 0], fin.at[y, x, 4 - k], line[k - 1]) for k in (1, 2, 3)]
    grads_out[...] = grads

    class Plane:
        def __init__(self, slots):
            self.slots = slots

        def at(self, yy, xx, start=0, size=128):
            return fin.at[yy, xx, self.slots, pl.ds(start, size)]

        def begin(self):
            a, b = self.at(y, x, 0, 64), self.at(y, x, 64, 64)
            self.ax = [share(a, to) for to in (right, left, across_x)]
            self.by = [share(b, to) for to in (up, down, across_y)]
            self.own = [share(a, up), share(b, right), share(a, down), share(b, left)]

        def turn(self):
            self.a, self.b = [], []
            for n, (xx, yy) in enumerate(((xd, yd), (xu, yu), (x2, y2))):
                arrived(self.ax[n])
                self.a.append([share(self.at(y, xx, 0, 64), to) for to in (up, down)])
                arrived(self.by[n])
                self.b.append([share(self.at(yy, x, 64, 64), to) for to in (right, left)])

        def forward(self):
            self.last = []
            au, br, ad, bl = self.own
            pairs = [(x, y, (au, ad), (br, bl))]
            pairs += zip((xd, xu, x2), (yd, yu, y2), self.a, self.b)
            for xx, yy, a, b in pairs:
                arrived(a[0])
                self.last.append(share(self.at(yd, xx, 0, 32), up))
                arrived(b[0])
                self.last.append(share(self.at(yy, xd, 64, 32), right))
                arrived(a[1])
                self.last.append(share(self.at(yu, xx, 32, 32), down))
                arrived(b[1])
                self.last.append(share(self.at(yy, xu, 96, 32), left))

        def end(self):
            arrived(*self.last)

    def unpack(r):
        n = (z + r) % 4
        columns = pl.ds(pl.multiple_of(n * 1280, 128), 1280)
        both = fin[:, :, r, 0:80, :].reshape(1280, 128).T
        weights_out[0, :, columns] = both[0:64]
        weights_out[1, :, columns] = both[64:128]
        folded = fin[:, :, r, 80:128, :].reshape(768, 128).astype(f32)
        rest = pltpu.roll(folded, 64, 1).reshape(16, 48, 128)[:, 0:32]
        third = jnp.concatenate([folded.reshape(16, 48, 128), rest], axis=1)
        weights_out[2, :, columns] = third.reshape(1280, 128).astype(bf16).T[0:64]

    one, two, rest = Plane(pl.ds(0, 1)), Plane(pl.ds(1, 1)), Plane(pl.ds(2, 2))
    one.begin()
    one.turn()
    arrived(c_z[2])
    two.begin()
    one.forward()
    arrived(c_z[0], c_z[1])
    rest.begin()
    two.turn()
    one.end()
    unpack(0)
    rest.turn()
    two.forward()
    rest.forward()
    two.end()
    unpack(1)
    rest.end()
    if stop == 10:
        return finish()
    unpack(2)
    unpack(3)
    finish()


def local(stop, inputs, upstream, master, moment_one, moment_two):
    hbm = pl.BlockSpec(memory_space=pltpu.HBM)
    vmem = pl.BlockSpec(memory_space=pltpu.VMEM)
    operands = (inputs, upstream, master, moment_one, moment_two)
    operands = [pltpu.with_memory_space_constraint(a, pltpu.HBM) for a in operands]
    grads, weights = pl.pallas_call(
        functools.partial(kernel, stop),
        out_shape=(pltpu.VMEM((3, 64, 80), f32), pltpu.VMEM((3, 64, 5120), bf16)),
        in_specs=[hbm] * 5,
        out_specs=(vmem,) * 2,
        scratch_shapes=[
            pltpu.VMEM((2, 4, 2, 128, 640), bf16),
            pltpu.VMEM((3, 3, 64, 80), f32),
            pltpu.VMEM((128, 128), bf16),
            pltpu.VMEM((4, 4, 128, 128), bf16),
            pltpu.VMEM((4, 192, 128), f32),
            pltpu.VMEM((192, 128), f32),
            pltpu.VMEM((2, 192, 128), f32),
            pltpu.VMEM((4, 192, 128), bf16),
            pltpu.VMEM((2, 4, 320, 512), bf16),
            pltpu.VMEM((4, 4, 120, 128), f32),
            pltpu.VMEM((4, 120, 128), f32),
            pltpu.VMEM((2, 4, 120, 128), f32),
            pltpu.VMEM((4, 120, 128), f32),
            pltpu.VMEM((3, 120, 128), f32),
            pltpu.VMEM((120, 128), f32),
            pltpu.VMEM((4, 4, 4, 128, 128), bf16),
            pltpu.SemaphoreType.DMA((N_COPIES,)),
            pltpu.SemaphoreType.DMA((N_COPIES,)),
            pltpu.SemaphoreType.DMA((5,)),
        ],
        compiler_params=pltpu.CompilerParams(
            collective_id=0, has_side_effects=True, vmem_limit_bytes=44 * 2**20
        ),
        cost_estimate=pl.CostEstimate(
            flops=503316480, bytes_accessed=8000000, transcendentals=8192
        ),
        name="fused_step",
    )(*operands)
    first, second, fresh = adamw(grads, master, moment_one, moment_two)
    return fresh, first, second, weights


def solution(mesh, stop=0):
    owned = P(None, "mp", "dp")
    return jax.shard_map(
        functools.partial(local, stop),
        mesh=mesh,
        in_specs=(P("dp", "mp"), P("dp", "mp"), owned, owned, owned),
        out_specs=(owned, owned, owned, P(None, "mp", None)),
        check_vma=False,
    )
```

```python
import jax
import jax.numpy as jnp
from jax import lax
from jax.experimental import pallas as pl
from jax.experimental.pallas import tpu as pltpu
from jax.sharding import PartitionSpec as P

beta_one = 0.9
beta_two = 0.95
learn_rate = 0.0003
decay_rate = 0.1
eps_small = 1e-08
corr_one = 1.0 - 0.9**40
corr_two = 1.0 - 0.95**40

MESH = pl.DeviceIdType.MESH
f32 = jnp.float32
bf16 = jnp.bfloat16
N_COPIES = 208


def adamw(grads, master, moment_one, moment_two):
    first = beta_one * moment_one + (1.0 - beta_one) * grads
    second = beta_two * moment_two + (1.0 - beta_two) * grads * grads
    update = first / corr_one / (jnp.sqrt(second / corr_two) + eps_small)
    return first, second, master - learn_rate * (update + decay_rate * master)


def kernel(
    inputs_hbm, upstream_hbm, master_hbm, moment_one_hbm, moment_two_hbm,
    grads_out, weights_out,
    feats, state, wown, wbuf, quarter, rs_half, rs_full, dcat,
    featT, gbuf, gy_half, gy_full, gline, gz_in, gin, fin,
    send_sems, recv_sems, load_sems,
):
    i, j = lax.axis_index("dp"), lax.axis_index("mp")
    z, y, x = i // 16, (i // 4) % 4, i % 4
    zh, core = j // 2, j % 2

    def dev(zh=zh, core=core, z=z, y=y, x=x):
        return (z * 16 + y * 4 + x, zh * 2 + core)

    flip = lambda v: v + 1 - 2 * (v % 2)
    xu, xd, x2 = (x + 1) % 4, (x + 3) % 4, (x + 2) % 4
    yu, yd, y2 = (y + 1) % 4, (y + 3) % 4, (y + 2) % 4
    zu, zd, z2 = (zh + 1) % 4, (zh + 3) % 4, (zh + 2) % 4
    right, left, up, down = dev(x=xu), dev(x=xd), dev(y=yu), dev(y=yd)
    across_x, across_y = dev(x=x2), dev(y=y2)
    line = [dev(z=(z + k) % 4) for k in (1, 2, 3)]
    skew = [dev(z=(z + k) % 4, x=(x + k) % 4) for k in (1, 2, 3)]
    above, below = dev(zh=zu), dev(zh=zd)
    mate = dev(core=1 - core)
    holders = [
        dev(zh=z, z=(x + m) % 4, y=flip(y), x=(zh + x + m) % 4) for m in range(4)
    ]
    owners = [
        dev(zh=(x + 4 - z) % 4, z=zh, y=flip(y), x=(z + 4 - m) % 4) for m in range(4)
    ]

    started = []

    def put(src, dst, to):
        k = len(started)
        copy = pltpu.make_async_remote_copy(
            src_ref=src, dst_ref=dst, send_sem=send_sems.at[k], recv_sem=recv_sems.at[k],
            device_id=to, device_id_type=MESH,
        )
        copy.start()
        started.append(copy)
        return copy

    def share(ref, to):
        return put(ref, ref, to)

    def arrived(*copies):
        for copy in copies:
            copy.wait_recv()

    def finish():
        for copy in started:
            copy.wait_send()

    barrier = pltpu.get_barrier_semaphore()
    greeted = [
        *holders, *owners, above, below, *line, *skew,
        right, left, up, down, across_x, across_y, mate,
    ]
    for other in greeted:
        pl.semaphore_signal(barrier, inc=1, device_id=other, device_id_type=MESH)

    loads = [
        pltpu.make_async_copy(src, dst, load_sems.at[k])
        for k, (src, dst) in enumerate([
            (master_hbm, state.at[0]),
            (inputs_hbm, feats.at[0, 0, core]),
            (upstream_hbm, feats.at[1, 0, core]),
            (moment_one_hbm, state.at[1]),
            (moment_two_hbm, state.at[2]),
        ])
    ]
    for load in loads:
        load.start()

    def low_lanes(n):
        return lax.broadcasted_iota(jnp.int32, (n, 128), 1) < 64

    def shard_block(rows):
        down_cols = jnp.concatenate([rows[128:192], jnp.zeros((64, 80), f32)], axis=0).T
        rest = jnp.concatenate([down_cols[48:80], jnp.zeros((16, 128), f32)], axis=0)
        folded = down_cols[0:48] + pltpu.roll(rest, 64, 1)
        return jnp.concatenate([rows[0:128].T, folded], axis=0).astype(bf16)

    loads[0].wait()
    wown[...] = shard_block(state[0].reshape(192, 80))
    for load in loads[1:]:
        load.wait()

    pl.semaphore_wait(barrier, len(greeted))

    gate_up, down_part = pl.ds(0, 80), pl.ds(80, 48)
    c_w = [
        [put(wown.at[rows], wbuf.at[y, x, rows], to) for to in holders]
        for rows in (gate_up, down_part)
    ]
    own = [feats.at[n, 0, core] for n in (0, 1)]
    c_r, c_l = [], []
    for n in (0, 1):
        c_r.append(put(own[n], feats.at[n, 3, core], right))
        c_l.append(put(own[n], feats.at[n, 1, core], left))
    c_m = [[share(own[n], mate)] for n in (0, 1)]
    c_y = [[], []]

    def spread(n, m):
        arrived(c_w[n][m])
        piece = wbuf.at[flip(y), (z + 4 - m) % 4, (gate_up, down_part)[n]]
        c_y[n].extend(share(piece, to) for to in (up, down, across_y))

    spread(0, 0)
    spread(0, 1)
    arrived(c_r[0])
    c_r2 = put(feats.at[0, 3, core], feats.at[0, 2, core], right)
    c_m[0].append(share(feats.at[0, 3, core], mate))
    spread(0, 2)
    spread(0, 3)
    arrived(c_l[0])
    c_m[0].append(share(feats.at[0, 1, core], mate))
    arrived(c_l[1])
    c_l2 = put(feats.at[1, 1, core], feats.at[1, 2, core], left)
    c_m[1].append(share(feats.at[1, 1, core], mate))
    for m in range(4):
        spread(1, m)
    arrived(c_r[1])
    c_m[1].append(share(feats.at[1, 3, core], mate))
    arrived(c_r2)
    c_m[0].append(share(feats.at[0, 2, core], mate))
    arrived(c_l2)
    c_m[1].append(share(feats.at[1, 2, core], mate))
    arrived(*c_m[0], *c_y[0])

    w01 = wbuf[:, :, 0:80, :].reshape(1280, 128)
    w01 = (w01[0:640], w01[640:1280])

    def forward01(q):
        p01 = jnp.dot(feats[0, q, 0], w01[0], preferred_element_type=f32)
        p01 += jnp.dot(feats[0, q, 1], w01[1], preferred_element_type=f32)
        quarter[q, 0:128] = p01

    def forward2(q):
        p2 = jnp.dot(feats[1, q, 0], w2[0], preferred_element_type=f32)
        p2 += jnp.dot(feats[1, q, 1], w2[1], preferred_element_type=f32)
        quarter[q, 128:192] = p2[0:64] + pltpu.roll(p2[64:128], 64, 1)

    lo, hi = (pl.ds(0, 64), pl.ds(128, 32)), (pl.ds(64, 64), pl.ds(160, 32))

    def opposite(n):
        return (
            put(quarter.at[z2, lo[n]], rs_half.at[lo[n]], above),
            put(quarter.at[z2, hi[n]], rs_half.at[hi[n]], below),
        )

    def direct(n):
        return (
            put(quarter.at[zu, hi[n]], rs_full.at[0, hi[n]], above),
            put(quarter.at[zd, lo[n]], rs_full.at[1, lo[n]], below),
        )

    def onward(n, c_a, c_b):
        arrived(c_a)
        quarter[zu, lo[n]] += rs_half[lo[n]]
        c_up = put(quarter.at[zu, lo[n]], rs_full.at[0, lo[n]], above)
        arrived(c_b)
        quarter[zd, hi[n]] += rs_half[hi[n]]
        return c_up, put(quarter.at[zd, hi[n]], rs_full.at[1, hi[n]], below)

    forward01(z2)
    c_o1 = opposite(0)
    forward01(zu)
    forward01(zd)
    arrived(*c_m[1], *c_y[1])
    folded = wbuf[:, :, 80:128, :].reshape(768, 128).astype(f32)
    low = low_lanes(768)
    first_rows = jnp.where(low, folded, 0.0).astype(bf16).reshape(16, 48, 128)
    last_rows = jnp.where(low, pltpu.roll(folded, 64, 1), 0.0).astype(bf16).reshape(16, 48, 128)
    w2 = jnp.concatenate([first_rows, last_rows[:, 0:32]], axis=1).reshape(1280, 128)
    w2 = (w2[0:640], w2[640:1280])
    forward2(z2)
    c_o2 = opposite(1)
    c_d = [*direct(0)]
    forward2(zu)
    forward2(zd)
    c_d += direct(1)
    forward01(zh)
    forward2(zh)
    c_d += onward(0, *c_o1)
    c_d += onward(1, *c_o2)
    for n in (0, 1):
        for q in range(4):
            for d in (0, 1):
                block = feats[n, q, d].T.reshape(2, 320, 128)
                featT[n, 2 * d : 2 * d + 2, :, 128 * q : 128 * q + 128] = block
    arrived(*c_d)

    total = quarter[zh] + rs_full[0] + rs_full[1]
    gate = total[0:128]
    upval = pltpu.roll(gate, 64, 1)
    dhidden = jnp.concatenate([total[128:192], pltpu.roll(total[128:192], 64, 1)], axis=0)
    sigma = jax.nn.sigmoid(gate)
    hidden = gate * sigma * upval
    dgate = dhidden * upval * sigma * (1.0 + gate * (1.0 - sigma))
    dup = dhidden * gate * sigma
    low = low_lanes(128)
    dcat[zh, 0:128] = jnp.where(low, dgate, pltpu.roll(dup, 64, 1)).astype(bf16)
    hidden = jnp.where(low[0:64], hidden[0:64], pltpu.roll(hidden[64:128], 64, 1))
    dcat[zh, 128:192] = hidden.astype(bf16)

    lo, hi = pl.ds(0, 96), pl.ds(96, 96)
    c_a1, c_b1 = share(dcat.at[zh, lo], above), share(dcat.at[zh, hi], below)
    c_a2, c_b2 = share(dcat.at[zh, hi], above), share(dcat.at[zh, lo], below)
    arrived(c_a1)
    c_a3 = share(dcat.at[zd, lo], above)
    arrived(c_b1)
    c_b3 = share(dcat.at[zu, hi], below)
    arrived(c_a2, c_b2, c_a3, c_b3)

    d01 = dcat[:, 0:128, :].reshape(512, 128)
    low = low_lanes(256)
    folded = dcat[:, 128:192, :].reshape(256, 128).astype(f32)
    early = jnp.where(low, folded, 0.0).astype(bf16).reshape(4, 64, 128)
    late = jnp.where(low, pltpu.roll(folded, 64, 1), 0.0).astype(bf16).reshape(4, 64, 128)
    d2 = jnp.concatenate([early, late], axis=1).reshape(512, 128)

    def backward(v):
        p01 = jnp.dot(featT[0, v], d01, preferred_element_type=f32)
        p2 = jnp.dot(featT[1, v], d2, preferred_element_type=f32).reshape(4, 80, 128)
        rest = pltpu.roll(p2[:, 40:80].reshape(160, 128), 64, 1).reshape(4, 40, 128)
        p01, p2 = p01.reshape(4, 80, 128), p2[:, 0:40] + rest
        for n in range(4):
            k = (n + 4 - z) % 4
            gbuf[v, k, 0:80] = p01[n]
            gbuf[v, k, 80:120] = p2[n]

    lo, hi = pl.ds(0, 2), pl.ds(2, 2)
    backward(flip(y2))
    c_o = [
        put(gbuf.at[flip(y2), k], gy_half.at[k], up if k < 2 else down) for k in range(4)
    ]
    backward(flip(yu))
    c_d = [put(gbuf.at[flip(yu), hi], gy_full.at[0, hi], up)]
    backward(flip(yd))
    c_d.append(put(gbuf.at[flip(yd), lo], gy_full.at[1, lo], down))
    backward(flip(y))
    c_f = [None] * 4
    for k in (1, 2, 3, 0):
        arrived(c_o[k])
        v = flip(yu) if k < 2 else flip(yd)
        gbuf[v, k] += gy_half[k]
        c_f[k] = put(gbuf.at[v, k], gy_full.at[k // 2, k], up if k < 2 else down)
    arrived(*c_d)
    c_z = []
    for k in (1, 2, 3, 0):
        arrived(c_f[k])
        gline[k] = gbuf[flip(y), k] + gy_full[0, k] + gy_full[1, k]
        if k > 0:
            c_z.append(put(gline.at[k], gz_in.at[k - 1], skew[k - 1]))
    arrived(*c_z)
    gline[0] += gz_in[0] + gz_in[1] + gz_in[2]

    arrived(put(gline.at[0], gin, owners[0]))

    g01 = gin[0:80]
    g2 = jnp.concatenate([gin[80:120], pltpu.roll(gin[80:120], 64, 1)], axis=0)
    grads = jnp.concatenate([g01.T, g2.T[0:64]], axis=0).reshape(3, 64, 80)
    fresh = adamw(grads, state[0], state[1], state[2])[2]
    fin[y, x, 0] = shard_block(fresh.reshape(192, 80))

    c_z = [put(fin.at[y, x, 0], fin.at[y, x, 4 - k], line[k - 1]) for k in (1, 2, 3)]
    grads_out[...] = grads

    class Plane:
        def __init__(self, slots):
            self.slots = slots

        def at(self, yy, xx, start=0, size=128):
            return fin.at[yy, xx, self.slots, pl.ds(start, size)]

        def begin(self):
            a, b = self.at(y, x, 0, 64), self.at(y, x, 64, 64)
            self.ax = [share(a, to) for to in (right, left, across_x)]
            self.by = [share(b, to) for to in (up, down, across_y)]
            self.own = [share(a, up), share(b, right), share(a, down), share(b, left)]

        def turn(self):
            self.a, self.b = [], []
            for n, (xx, yy) in enumerate(((xd, yd), (xu, yu), (x2, y2))):
                arrived(self.ax[n])
                self.a.append([share(self.at(y, xx, 0, 64), to) for to in (up, down)])
                arrived(self.by[n])
                self.b.append([share(self.at(yy, x, 64, 64), to) for to in (right, left)])

        def forward(self):
            self.last = []
            au, br, ad, bl = self.own
            pairs = [(x, y, (au, ad), (br, bl))]
            pairs += zip((xd, xu, x2), (yd, yu, y2), self.a, self.b)
            for xx, yy, a, b in pairs:
                arrived(a[0])
                self.last.append(share(self.at(yd, xx, 0, 32), up))
                arrived(b[0])
                self.last.append(share(self.at(yy, xd, 64, 32), right))
                arrived(a[1])
                self.last.append(share(self.at(yu, xx, 32, 32), down))
                arrived(b[1])
                self.last.append(share(self.at(yy, xu, 96, 32), left))

        def end(self):
            arrived(*self.last)

    def unpack(r):
        n = (z + r) % 4
        columns = pl.ds(pl.multiple_of(n * 1280, 128), 1280)
        both = fin[:, :, r, 0:80, :].reshape(1280, 128).T
        weights_out[0, :, columns] = both[0:64]
        weights_out[1, :, columns] = both[64:128]
        folded = fin[:, :, r, 80:128, :].reshape(768, 128).astype(f32)
        rest = pltpu.roll(folded, 64, 1).reshape(16, 48, 128)[:, 0:32]
        third = jnp.concatenate([folded.reshape(16, 48, 128), rest], axis=1)
        weights_out[2, :, columns] = third.reshape(1280, 128).astype(bf16).T[0:64]

    near, far = Plane(pl.ds(0, 1)), Plane(pl.ds(1, 3))
    near.begin()
    near.turn()
    arrived(*c_z)
    far.begin()
    near.forward()
    far.turn()
    near.end()
    far.forward()
    unpack(0)
    far.end()
    for r in (1, 2, 3):
        unpack(r)
    finish()


def local(inputs, upstream, master, moment_one, moment_two):
    hbm = pl.BlockSpec(memory_space=pltpu.HBM)
    vmem = pl.BlockSpec(memory_space=pltpu.VMEM)
    operands = (inputs, upstream, master, moment_one, moment_two)
    operands = [pltpu.with_memory_space_constraint(a, pltpu.HBM) for a in operands]
    grads, weights = pl.pallas_call(
        kernel,
        out_shape=(pltpu.VMEM((3, 64, 80), f32), pltpu.VMEM((3, 64, 5120), bf16)),
        in_specs=[hbm] * 5,
        out_specs=(vmem,) * 2,
        scratch_shapes=[
            pltpu.VMEM((2, 4, 2, 128, 640), bf16),
            pltpu.VMEM((3, 3, 64, 80), f32),
            pltpu.VMEM((128, 128), bf16),
            pltpu.VMEM((4, 4, 128, 128), bf16),
            pltpu.VMEM((4, 192, 128), f32),
            pltpu.VMEM((192, 128), f32),
            pltpu.VMEM((2, 192, 128), f32),
            pltpu.VMEM((4, 192, 128), bf16),
            pltpu.VMEM((2, 4, 320, 512), bf16),
            pltpu.VMEM((4, 4, 120, 128), f32),
            pltpu.VMEM((4, 120, 128), f32),
            pltpu.VMEM((2, 4, 120, 128), f32),
            pltpu.VMEM((4, 120, 128), f32),
            pltpu.VMEM((3, 120, 128), f32),
            pltpu.VMEM((120, 128), f32),
            pltpu.VMEM((4, 4, 4, 128, 128), bf16),
            pltpu.SemaphoreType.DMA((N_COPIES,)),
            pltpu.SemaphoreType.DMA((N_COPIES,)),
            pltpu.SemaphoreType.DMA((5,)),
        ],
        compiler_params=pltpu.CompilerParams(
            collective_id=0, has_side_effects=True, vmem_limit_bytes=44 * 2**20
        ),
        cost_estimate=pl.CostEstimate(
            flops=503316480, bytes_accessed=8000000, transcendentals=8192
        ),
        name="fused_step",
    )(*operands)
    first, second, fresh = adamw(grads, master, moment_one, moment_two)
    return fresh, first, second, weights


def solution(mesh):
    owned = P(None, "mp", "dp")
    return jax.shard_map(
        local,
        mesh=mesh,
        in_specs=(P("dp", "mp"), P("dp", "mp"), owned, owned, owned),
        out_specs=(owned, owned, owned, P(None, "mp", None)),
        check_vma=False,
    )
```

```python
import jax
import jax.numpy as jnp
from jax import lax
from jax.experimental import pallas as pl
from jax.experimental.pallas import tpu as pltpu
from jax.sharding import PartitionSpec as P

beta_one = 0.9
beta_two = 0.95
learn_rate = 0.0003
decay_rate = 0.1
eps_small = 1e-08
corr_one = 1.0 - 0.9**40
corr_two = 1.0 - 0.95**40

MESH = pl.DeviceIdType.MESH
f32 = jnp.float32
bf16 = jnp.bfloat16
N_COPIES = 208


def adamw(grads, master, moment_one, moment_two):
    first = beta_one * moment_one + (1.0 - beta_one) * grads
    second = beta_two * moment_two + (1.0 - beta_two) * grads * grads
    update = first / corr_one / (jnp.sqrt(second / corr_two) + eps_small)
    return first, second, master - learn_rate * (update + decay_rate * master)


def kernel(
    inputs_hbm, upstream_hbm, master_hbm, moment_one_hbm, moment_two_hbm,
    grads_out, weights_out,
    feats, state, wown, wbuf, quarter, rs_half, rs_full, dcat,
    featT, gbuf, gy_half, gy_full, gline, gz_in, gin, fin,
    send_sems, recv_sems, load_sems,
):
    i, j = lax.axis_index("dp"), lax.axis_index("mp")
    z, y, x = i // 16, (i // 4) % 4, i % 4
    zh, core = j // 2, j % 2

    def dev(zh=zh, core=core, z=z, y=y, x=x):
        return (z * 16 + y * 4 + x, zh * 2 + core)

    flip = lambda v: v + 1 - 2 * (v % 2)
    xu, xd, x2 = (x + 1) % 4, (x + 3) % 4, (x + 2) % 4
    yu, yd, y2 = (y + 1) % 4, (y + 3) % 4, (y + 2) % 4
    zu, zd, z2 = (zh + 1) % 4, (zh + 3) % 4, (zh + 2) % 4
    right, left, up, down = dev(x=xu), dev(x=xd), dev(y=yu), dev(y=yd)
    across_x, across_y = dev(x=x2), dev(y=y2)
    line = [dev(z=(z + k) % 4) for k in (1, 2, 3)]
    skew = [dev(z=(z + k) % 4, x=(x + k) % 4) for k in (1, 2, 3)]
    above, below = dev(zh=zu), dev(zh=zd)
    mate = dev(core=1 - core)
    holders = [
        dev(zh=z, z=(x + m) % 4, y=flip(y), x=(zh + x + m) % 4) for m in range(4)
    ]
    owners = [
        dev(zh=(x + 4 - z) % 4, z=zh, y=flip(y), x=(z + 4 - m) % 4) for m in range(4)
    ]

    started = []

    def put(src, dst, to):
        k = len(started)
        copy = pltpu.make_async_remote_copy(
            src_ref=src, dst_ref=dst, send_sem=send_sems.at[k], recv_sem=recv_sems.at[k],
            device_id=to, device_id_type=MESH,
        )
        copy.start()
        started.append(copy)
        return copy

    def share(ref, to):
        return put(ref, ref, to)

    def arrived(*copies):
        for copy in copies:
            copy.wait_recv()

    def finish():
        for copy in started:
            copy.wait_send()

    barrier = pltpu.get_barrier_semaphore()
    greeted = [
        *holders, *owners, above, below, *line, *skew,
        right, left, up, down, across_x, across_y, mate,
    ]
    for other in greeted:
        pl.semaphore_signal(barrier, inc=1, device_id=other, device_id_type=MESH)

    loads = [
        pltpu.make_async_copy(src, dst, load_sems.at[k])
        for k, (src, dst) in enumerate([
            (master_hbm, state.at[0]),
            (inputs_hbm, feats.at[0, 0, core]),
            (upstream_hbm, feats.at[1, 0, core]),
            (moment_one_hbm, state.at[1]),
            (moment_two_hbm, state.at[2]),
        ])
    ]
    for load in loads:
        load.start()

    def low_lanes(n):
        return lax.broadcasted_iota(jnp.int32, (n, 128), 1) < 64

    def shard_block(rows):
        down_cols = jnp.concatenate([rows[128:192], jnp.zeros((64, 80), f32)], axis=0).T
        rest = jnp.concatenate([down_cols[48:80], jnp.zeros((16, 128), f32)], axis=0)
        folded = down_cols[0:48] + pltpu.roll(rest, 64, 1)
        return jnp.concatenate([rows[0:128].T, folded], axis=0).astype(bf16)

    loads[0].wait()
    wown[...] = shard_block(state[0].reshape(192, 80))
    for load in loads[1:]:
        load.wait()

    pl.semaphore_wait(barrier, len(greeted))

    gate_up, down_part = pl.ds(0, 80), pl.ds(80, 48)
    c_w = [
        [put(wown.at[rows], wbuf.at[y, x, rows], to) for to in holders]
        for rows in (gate_up, down_part)
    ]
    own = [feats.at[n, 0, core] for n in (0, 1)]
    c_r, c_l = [], []
    for n in (0, 1):
        c_r.append(put(own[n], feats.at[n, 3, core], right))
        c_l.append(put(own[n], feats.at[n, 1, core], left))
    c_m = [[share(own[n], mate)] for n in (0, 1)]
    c_y = [[], []]

    def spread(n, m):
        arrived(c_w[n][m])
        piece = wbuf.at[flip(y), (z + 4 - m) % 4, (gate_up, down_part)[n]]
        c_y[n].extend(share(piece, to) for to in (up, down, across_y))

    spread(0, 0)
    spread(0, 1)
    arrived(c_r[0])
    c_r2 = put(feats.at[0, 3, core], feats.at[0, 2, core], right)
    c_m[0].append(share(feats.at[0, 3, core], mate))
    spread(0, 2)
    spread(0, 3)
    arrived(c_l[0])
    c_m[0].append(share(feats.at[0, 1, core], mate))
    arrived(c_l[1])
    c_l2 = put(feats.at[1, 1, core], feats.at[1, 2, core], left)
    c_m[1].append(share(feats.at[1, 1, core], mate))
    for m in range(4):
        spread(1, m)
    arrived(c_r[1])
    c_m[1].append(share(feats.at[1, 3, core], mate))
    arrived(c_r2)
    c_m[0].append(share(feats.at[0, 2, core], mate))
    arrived(c_l2)
    c_m[1].append(share(feats.at[1, 2, core], mate))
    arrived(*c_m[0], *c_y[0])

    w01 = wbuf[:, :, 0:80, :].reshape(1280, 128)
    w01 = (w01[0:640], w01[640:1280])

    def forward01(q):
        p01 = jnp.dot(feats[0, q, 0], w01[0], preferred_element_type=f32)
        p01 += jnp.dot(feats[0, q, 1], w01[1], preferred_element_type=f32)
        quarter[q, 0:128] = p01

    def forward2(q):
        p2 = jnp.dot(feats[1, q, 0], w2[0], preferred_element_type=f32)
        p2 += jnp.dot(feats[1, q, 1], w2[1], preferred_element_type=f32)
        quarter[q, 128:192] = p2[0:64] + pltpu.roll(p2[64:128], 64, 1)

    lo, hi = (pl.ds(0, 64), pl.ds(128, 32)), (pl.ds(64, 64), pl.ds(160, 32))

    def opposite(n):
        return (
            put(quarter.at[z2, lo[n]], rs_half.at[lo[n]], above),
            put(quarter.at[z2, hi[n]], rs_half.at[hi[n]], below),
        )

    def direct(n):
        return (
            put(quarter.at[zu, hi[n]], rs_full.at[0, hi[n]], above),
            put(quarter.at[zd, lo[n]], rs_full.at[1, lo[n]], below),
        )

    def onward(n, c_a, c_b):
        arrived(c_a)
        quarter[zu, lo[n]] += rs_half[lo[n]]
        c_up = put(quarter.at[zu, lo[n]], rs_full.at[0, lo[n]], above)
        arrived(c_b)
        quarter[zd, hi[n]] += rs_half[hi[n]]
        return c_up, put(quarter.at[zd, hi[n]], rs_full.at[1, hi[n]], below)

    forward01(z2)
    c_o1 = opposite(0)
    forward01(zu)
    forward01(zd)
    arrived(*c_m[1], *c_y[1])
    folded = wbuf[:, :, 80:128, :].reshape(768, 128).astype(f32)
    low = low_lanes(768)
    first_rows = jnp.where(low, folded, 0.0).astype(bf16).reshape(16, 48, 128)
    last_rows = jnp.where(low, pltpu.roll(folded, 64, 1), 0.0).astype(bf16).reshape(16, 48, 128)
    w2 = jnp.concatenate([first_rows, last_rows[:, 0:32]], axis=1).reshape(1280, 128)
    w2 = (w2[0:640], w2[640:1280])
    forward2(z2)
    c_o2 = opposite(1)
    c_d = [direct(0)]
    forward2(zu)
    forward2(zd)
    c_d.append(direct(1))
    forward01(zh)
    forward2(zh)
    c_d[0] += onward(0, *c_o1)
    c_d[1] += onward(1, *c_o2)
    for n in (0, 1):
        for q in range(4):
            for d in (0, 1):
                block = feats[n, q, d].T.reshape(2, 320, 128)
                featT[n, 2 * d : 2 * d + 2, :, 128 * q : 128 * q + 128] = block

    def summed(n, rows):
        arrived(*c_d[n])
        return quarter[zh, rows] + rs_full[0, rows] + rs_full[1, rows]

    def gather(n):
        mine, a, b = dcat.at[zh], lo[n], hi[n]
        pairs = ((a, above), (b, below), (b, above), (a, below))
        return [share(mine.at[rows], to) for rows, to in pairs]

    def pass_on(n, copies):
        arrived(copies[0])
        c_a = share(dcat.at[zd, lo[n]], above)
        arrived(copies[1])
        return [c_a, share(dcat.at[zu, hi[n]], below)]

    low = low_lanes(128)
    gate = summed(0, slice(0, 128))
    upval = pltpu.roll(gate, 64, 1)
    sigma = jax.nn.sigmoid(gate)
    hidden = gate * sigma * upval
    hidden = jnp.where(low[0:64], hidden[0:64], pltpu.roll(hidden[64:128], 64, 1))
    dcat[zh, 128:192] = hidden.astype(bf16)
    c_h = gather(1)
    folded = summed(1, slice(128, 192))
    dhidden = jnp.concatenate([folded, pltpu.roll(folded, 64, 1)], axis=0)
    dgate = dhidden * upval * sigma * (1.0 + gate * (1.0 - sigma))
    dup = dhidden * gate * sigma
    dcat[zh, 0:128] = jnp.where(low, dgate, pltpu.roll(dup, 64, 1)).astype(bf16)
    c_g = gather(0)
    c_h = c_h[2:] + pass_on(1, c_h)
    c_g = c_g[2:] + pass_on(0, c_g)

    lo, hi = pl.ds(0, 2), pl.ds(2, 2)
    wide, down_rows = pl.ds(0, 80), pl.ds(80, 40)

    def store(v, rows, values):
        for n in range(4):
            gbuf[v, (n + 4 - z) % 4, rows] = values[n]

    arrived(*c_h)
    low = low_lanes(256)
    folded = dcat[:, 128:192, :].reshape(256, 128).astype(f32)
    early = jnp.where(low, folded, 0.0).astype(bf16).reshape(4, 64, 128)
    late = jnp.where(low, pltpu.roll(folded, 64, 1), 0.0).astype(bf16).reshape(4, 64, 128)
    d2 = jnp.concatenate([early, late], axis=1).reshape(512, 128)

    def backward2(v):
        p2 = jnp.dot(featT[1, v], d2, preferred_element_type=f32).reshape(4, 80, 128)
        rest = pltpu.roll(p2[:, 40:80].reshape(160, 128), 64, 1).reshape(4, 40, 128)
        store(v, down_rows, p2[:, 0:40] + rest)

    backward2(flip(y2))
    h_o = [
        put(gbuf.at[flip(y2), lo, down_rows], gy_half.at[lo, down_rows], up),
        put(gbuf.at[flip(y2), hi, down_rows], gy_half.at[hi, down_rows], down),
    ]
    backward2(flip(yu))
    backward2(flip(yd))
    h_d = [
        put(gbuf.at[flip(yu), hi, down_rows], gy_full.at[0, hi, down_rows], up),
        put(gbuf.at[flip(yd), lo, down_rows], gy_full.at[1, lo, down_rows], down),
    ]
    backward2(flip(y))

    arrived(*c_g)
    d01 = dcat[:, 0:128, :].reshape(512, 128)

    def backward01(v):
        p01 = jnp.dot(featT[0, v], d01, preferred_element_type=f32)
        store(v, wide, p01.reshape(4, 80, 128))

    backward01(flip(y2))
    c_o = [
        put(gbuf.at[flip(y2), k, wide], gy_half.at[k, wide], up if k < 2 else down)
        for k in range(4)
    ]
    backward01(flip(yu))
    c_d = [put(gbuf.at[flip(yu), hi, wide], gy_full.at[0, hi, wide], up)]
    backward01(flip(yd))
    c_d.append(put(gbuf.at[flip(yd), lo, wide], gy_full.at[1, lo, wide], down))
    arrived(h_o[0])
    gbuf[flip(yu), lo, down_rows] += gy_half[lo, down_rows]
    h_d.append(put(gbuf.at[flip(yu), lo, down_rows], gy_full.at[0, lo, down_rows], up))
    arrived(h_o[1])
    gbuf[flip(yd), hi, down_rows] += gy_half[hi, down_rows]
    h_d.append(put(gbuf.at[flip(yd), hi, down_rows], gy_full.at[1, hi, down_rows], down))
    backward01(flip(y))
    c_f = [None] * 4
    for k in (1, 2, 3, 0):
        arrived(c_o[k])
        v = flip(yu) if k < 2 else flip(yd)
        gbuf[v, k, wide] += gy_half[k, wide]
        dst = gy_full.at[k // 2, k, wide]
        c_f[k] = put(gbuf.at[v, k, wide], dst, up if k < 2 else down)

    def along(k, rows):
        gline[k, rows] = gbuf[flip(y), k, rows] + gy_full[0, k, rows] + gy_full[1, k, rows]
        if k > 0:
            return put(gline.at[k, rows], gz_in.at[k - 1, rows], skew[k - 1])

    def home(copies, rows):
        arrived(*copies)
        gline[0, rows] += gz_in[0, rows] + gz_in[1, rows] + gz_in[2, rows]
        return put(gline.at[0, rows], gin.at[rows], owners[0])

    arrived(*h_d)
    h_z = [along(k, down_rows) for k in (1, 2, 3, 0)][:3]
    arrived(*c_d)
    c_z = []
    for k in (1, 2, 3, 0):
        arrived(c_f[k])
        c_z.append(along(k, wide))
    c_home = [home(h_z, down_rows), home(c_z[:3], wide)]
    arrived(*c_home)

    g01 = gin[0:80]
    g2 = jnp.concatenate([gin[80:120], pltpu.roll(gin[80:120], 64, 1)], axis=0)
    grads = jnp.concatenate([g01.T, g2.T[0:64]], axis=0).reshape(3, 64, 80)
    fresh = adamw(grads, state[0], state[1], state[2])[2]
    fin[y, x, 0] = shard_block(fresh.reshape(192, 80))

    c_z = [put(fin.at[y, x, 0], fin.at[y, x, 4 - k], line[k - 1]) for k in (1, 2, 3)]
    grads_out[...] = grads

    class Plane:
        def __init__(self, slots):
            self.slots = slots

        def at(self, yy, xx, start=0, size=128):
            return fin.at[yy, xx, self.slots, pl.ds(start, size)]

        def begin(self):
            a, b = self.at(y, x, 0, 64), self.at(y, x, 64, 64)
            self.ax = [share(a, to) for to in (right, left, across_x)]
            self.by = [share(b, to) for to in (up, down, across_y)]
            self.own = [share(a, up), share(b, right), share(a, down), share(b, left)]

        def turn(self):
            self.a, self.b = [], []
            for n, (xx, yy) in enumerate(((xd, yd), (xu, yu), (x2, y2))):
                arrived(self.ax[n])
                self.a.append([share(self.at(y, xx, 0, 64), to) for to in (up, down)])
                arrived(self.by[n])
                self.b.append([share(self.at(yy, x, 64, 64), to) for to in (right, left)])

        def forward(self):
            self.last = []
            au, br, ad, bl = self.own
            pairs = [(x, y, (au, ad), (br, bl))]
            pairs += zip((xd, xu, x2), (yd, yu, y2), self.a, self.b)
            for xx, yy, a, b in pairs:
                arrived(a[0])
                self.last.append(share(self.at(yd, xx, 0, 32), up))
                arrived(b[0])
                self.last.append(share(self.at(yy, xd, 64, 32), right))
                arrived(a[1])
                self.last.append(share(self.at(yu, xx, 32, 32), down))
                arrived(b[1])
                self.last.append(share(self.at(yy, xu, 96, 32), left))

        def end(self):
            arrived(*self.last)

    def unpack(r):
        n = (z + r) % 4
        columns = pl.ds(pl.multiple_of(n * 1280, 128), 1280)
        both = fin[:, :, r, 0:80, :].reshape(1280, 128).T
        weights_out[0, :, columns] = both[0:64]
        weights_out[1, :, columns] = both[64:128]
        folded = fin[:, :, r, 80:128, :].reshape(768, 128).astype(f32)
        rest = pltpu.roll(folded, 64, 1).reshape(16, 48, 128)[:, 0:32]
        third = jnp.concatenate([folded.reshape(16, 48, 128), rest], axis=1)
        weights_out[2, :, columns] = third.reshape(1280, 128).astype(bf16).T[0:64]

    near, far = Plane(pl.ds(0, 1)), Plane(pl.ds(1, 3))
    near.begin()
    near.turn()
    arrived(*c_z)
    far.begin()
    near.forward()
    far.turn()
    near.end()
    far.forward()
    unpack(0)
    far.end()
    for r in (1, 2, 3):
        unpack(r)
    finish()


def local(inputs, upstream, master, moment_one, moment_two):
    hbm = pl.BlockSpec(memory_space=pltpu.HBM)
    vmem = pl.BlockSpec(memory_space=pltpu.VMEM)
    operands = (inputs, upstream, master, moment_one, moment_two)
    operands = [pltpu.with_memory_space_constraint(a, pltpu.HBM) for a in operands]
    grads, weights = pl.pallas_call(
        kernel,
        out_shape=(pltpu.VMEM((3, 64, 80), f32), pltpu.VMEM((3, 64, 5120), bf16)),
        in_specs=[hbm] * 5,
        out_specs=(vmem,) * 2,
        scratch_shapes=[
            pltpu.VMEM((2, 4, 2, 128, 640), bf16),
            pltpu.VMEM((3, 3, 64, 80), f32),
            pltpu.VMEM((128, 128), bf16),
            pltpu.VMEM((4, 4, 128, 128), bf16),
            pltpu.VMEM((4, 192, 128), f32),
            pltpu.VMEM((192, 128), f32),
            pltpu.VMEM((2, 192, 128), f32),
            pltpu.VMEM((4, 192, 128), bf16),
            pltpu.VMEM((2, 4, 320, 512), bf16),
            pltpu.VMEM((4, 4, 120, 128), f32),
            pltpu.VMEM((4, 120, 128), f32),
            pltpu.VMEM((2, 4, 120, 128), f32),
            pltpu.VMEM((4, 120, 128), f32),
            pltpu.VMEM((3, 120, 128), f32),
            pltpu.VMEM((120, 128), f32),
            pltpu.VMEM((4, 4, 4, 128, 128), bf16),
            pltpu.SemaphoreType.DMA((N_COPIES,)),
            pltpu.SemaphoreType.DMA((N_COPIES,)),
            pltpu.SemaphoreType.DMA((5,)),
        ],
        compiler_params=pltpu.CompilerParams(
            collective_id=0, has_side_effects=True, vmem_limit_bytes=44 * 2**20
        ),
        cost_estimate=pl.CostEstimate(
            flops=503316480, bytes_accessed=8000000, transcendentals=8192
        ),
        name="fused_step",
    )(*operands)
    first, second, fresh = adamw(grads, master, moment_one, moment_two)
    return fresh, first, second, weights


def solution(mesh):
    owned = P(None, "mp", "dp")
    return jax.shard_map(
        local,
        mesh=mesh,
        in_specs=(P("dp", "mp"), P("dp", "mp"), owned, owned, owned),
        out_specs=(owned, owned, owned, P(None, "mp", None)),
        check_vma=False,
    )
```

```python
import jax
import jax.numpy as jnp
from jax import lax
from jax.experimental import pallas as pl
from jax.experimental.pallas import tpu as pltpu
from jax.sharding import PartitionSpec as P

beta_one = 0.9
beta_two = 0.95
learn_rate = 0.0003
decay_rate = 0.1
eps_small = 1e-08
corr_one = 1.0 - 0.9**40
corr_two = 1.0 - 0.95**40

MESH = pl.DeviceIdType.MESH
f32 = jnp.float32
bf16 = jnp.bfloat16
N_COPIES = 208


def adamw(grads, master, moment_one, moment_two):
    first = beta_one * moment_one + (1.0 - beta_one) * grads
    second = beta_two * moment_two + (1.0 - beta_two) * grads * grads
    update = first / corr_one / (jnp.sqrt(second / corr_two) + eps_small)
    return first, second, master - learn_rate * (update + decay_rate * master)


def kernel(
    inputs_hbm, upstream_hbm, master_hbm, moment_one_hbm, moment_two_hbm,
    grads_out, weights_out,
    feats, state, wown, wbuf, quarter, rs_half, rs_full, dcat,
    featT, gbuf, gy_half, gy_full, gline, gz_in, gin, fin,
    send_sems, recv_sems, load_sems,
):
    i, j = lax.axis_index("dp"), lax.axis_index("mp")
    z, y, x = i // 16, (i // 4) % 4, i % 4
    zh, core = j // 2, j % 2

    def dev(zh=zh, core=core, z=z, y=y, x=x):
        return (z * 16 + y * 4 + x, zh * 2 + core)

    flip = lambda v: v + 1 - 2 * (v % 2)
    xu, xd, x2 = (x + 1) % 4, (x + 3) % 4, (x + 2) % 4
    yu, yd, y2 = (y + 1) % 4, (y + 3) % 4, (y + 2) % 4
    zu, zd, z2 = (zh + 1) % 4, (zh + 3) % 4, (zh + 2) % 4
    right, left, up, down = dev(x=xu), dev(x=xd), dev(y=yu), dev(y=yd)
    across_x, across_y = dev(x=x2), dev(y=y2)
    line = [dev(z=(z + k) % 4) for k in (1, 2, 3)]
    skew = [dev(z=(z + k) % 4, x=(x + k) % 4) for k in (1, 2, 3)]
    above, below = dev(zh=zu), dev(zh=zd)
    mate = dev(core=1 - core)
    holders = [
        dev(zh=z, z=(x + m) % 4, y=flip(y), x=(zh + x + m) % 4) for m in range(4)
    ]
    owners = [
        dev(zh=(x + 4 - z) % 4, z=zh, y=flip(y), x=(z + 4 - m) % 4) for m in range(4)
    ]

    started = []

    def put(src, dst, to):
        k = len(started)
        copy = pltpu.make_async_remote_copy(
            src_ref=src, dst_ref=dst, send_sem=send_sems.at[k], recv_sem=recv_sems.at[k],
            device_id=to, device_id_type=MESH,
        )
        copy.start()
        started.append(copy)
        return copy

    def share(ref, to):
        return put(ref, ref, to)

    def arrived(*copies):
        for copy in copies:
            copy.wait_recv()

    def finish():
        for copy in started:
            copy.wait_send()

    barrier = pltpu.get_barrier_semaphore()
    greeted = [
        *holders, *owners, above, below, *line, *skew,
        right, left, up, down, across_x, across_y, mate,
    ]
    for other in greeted:
        pl.semaphore_signal(barrier, inc=1, device_id=other, device_id_type=MESH)

    loads = [
        pltpu.make_async_copy(src, dst, load_sems.at[k])
        for k, (src, dst) in enumerate([
            (master_hbm, state.at[0]),
            (inputs_hbm, feats.at[0, 0, core]),
            (upstream_hbm, feats.at[1, 0, core]),
            (moment_one_hbm, state.at[1]),
            (moment_two_hbm, state.at[2]),
        ])
    ]
    for load in loads:
        load.start()

    def low_lanes(n):
        return lax.broadcasted_iota(jnp.int32, (n, 128), 1) < 64

    def shard_block(rows):
        down_cols = jnp.concatenate([rows[128:192], jnp.zeros((64, 80), f32)], axis=0).T
        rest = jnp.concatenate([down_cols[48:80], jnp.zeros((16, 128), f32)], axis=0)
        folded = down_cols[0:48] + pltpu.roll(rest, 64, 1)
        return jnp.concatenate([rows[0:128].T, folded], axis=0).astype(bf16)

    loads[0].wait()
    wown[...] = shard_block(state[0].reshape(192, 80))
    for load in loads[1:]:
        load.wait()

    pl.semaphore_wait(barrier, len(greeted))

    gate_up, down_part = pl.ds(0, 80), pl.ds(80, 48)
    c_w = [
        [put(wown.at[rows], wbuf.at[y, x, rows], to) for to in holders]
        for rows in (gate_up, down_part)
    ]
    own = [feats.at[n, 0, core] for n in (0, 1)]
    c_r, c_l = [], []
    for n in (0, 1):
        c_r.append(put(own[n], feats.at[n, 3, core], right))
        c_l.append(put(own[n], feats.at[n, 1, core], left))
    c_m = [[share(own[n], mate)] for n in (0, 1)]
    c_y = [[], []]

    def spread(n, m):
        arrived(c_w[n][m])
        piece = wbuf.at[flip(y), (z + 4 - m) % 4, (gate_up, down_part)[n]]
        c_y[n].extend(share(piece, to) for to in (up, down, across_y))

    arrived(c_r[0])
    c_r2 = put(feats.at[0, 3, core], feats.at[0, 2, core], right)
    c_m[0].append(share(feats.at[0, 3, core], mate))
    arrived(c_l[0])
    c_m[0].append(share(feats.at[0, 1, core], mate))
    for m in range(4):
        spread(0, m)
    arrived(c_l[1])
    c_l2 = put(feats.at[1, 1, core], feats.at[1, 2, core], left)
    c_m[1].append(share(feats.at[1, 1, core], mate))
    for m in range(4):
        spread(1, m)
    arrived(c_r2)
    c_m[0].append(share(feats.at[0, 2, core], mate))
    arrived(c_r[1])
    c_m[1].append(share(feats.at[1, 3, core], mate))
    arrived(*c_m[0], *c_y[0])

    w01 = wbuf[:, :, 0:80, :].reshape(1280, 128)
    w01 = (w01[0:640], w01[640:1280])

    def forward01(q):
        p01 = jnp.dot(feats[0, q, 0], w01[0], preferred_element_type=f32)
        p01 += jnp.dot(feats[0, q, 1], w01[1], preferred_element_type=f32)
        quarter[q, 0:128] = p01

    def forward2(q):
        p2 = jnp.dot(feats[1, q, 0], w2[0], preferred_element_type=f32)
        p2 += jnp.dot(feats[1, q, 1], w2[1], preferred_element_type=f32)
        quarter[q, 128:192] = p2[0:64] + pltpu.roll(p2[64:128], 64, 1)

    lo, hi = (pl.ds(0, 64), pl.ds(128, 32)), (pl.ds(64, 64), pl.ds(160, 32))

    def opposite(n):
        return (
            put(quarter.at[z2, lo[n]], rs_half.at[lo[n]], above),
            put(quarter.at[z2, hi[n]], rs_half.at[hi[n]], below),
        )

    def direct(n):
        return (
            put(quarter.at[zu, hi[n]], rs_full.at[0, hi[n]], above),
            put(quarter.at[zd, lo[n]], rs_full.at[1, lo[n]], below),
        )

    def onward(n, c_a, c_b):
        arrived(c_a)
        quarter[zu, lo[n]] += rs_half[lo[n]]
        c_up = put(quarter.at[zu, lo[n]], rs_full.at[0, lo[n]], above)
        arrived(c_b)
        quarter[zd, hi[n]] += rs_half[hi[n]]
        return c_up, put(quarter.at[zd, hi[n]], rs_full.at[1, hi[n]], below)

    forward01(z2)
    c_o1 = opposite(0)
    forward01(zu)
    forward01(zd)
    arrived(c_l2)
    c_m[1].append(share(feats.at[1, 2, core], mate))
    arrived(*c_m[1], *c_y[1])
    folded = wbuf[:, :, 80:128, :].reshape(768, 128).astype(f32)
    low = low_lanes(768)
    first_rows = jnp.where(low, folded, 0.0).astype(bf16).reshape(16, 48, 128)
    last_rows = jnp.where(low, pltpu.roll(folded, 64, 1), 0.0).astype(bf16).reshape(16, 48, 128)
    w2 = jnp.concatenate([first_rows, last_rows[:, 0:32]], axis=1).reshape(1280, 128)
    w2 = (w2[0:640], w2[640:1280])
    forward2(z2)
    c_o2 = opposite(1)
    c_d = [direct(0)]
    forward2(zu)
    forward2(zd)
    c_d.append(direct(1))
    forward01(zh)
    forward2(zh)
    c_d[0] += onward(0, *c_o1)
    c_d[1] += onward(1, *c_o2)
    for n in (0, 1):
        for q in range(4):
            for d in (0, 1):
                block = feats[n, q, d].T.reshape(2, 320, 128)
                featT[n, 2 * d : 2 * d + 2, :, 128 * q : 128 * q + 128] = block

    def summed(n, rows):
        arrived(*c_d[n])
        return quarter[zh, rows] + rs_full[0, rows] + rs_full[1, rows]

    def gather(n):
        mine, a, b = dcat.at[zh], lo[n], hi[n]
        pairs = ((a, above), (b, below), (b, above), (a, below))
        return [share(mine.at[rows], to) for rows, to in pairs]

    def pass_on(n, copies):
        arrived(copies[0])
        c_a = share(dcat.at[zd, lo[n]], above)
        arrived(copies[1])
        return [c_a, share(dcat.at[zu, hi[n]], below)]

    low = low_lanes(128)
    gate = summed(0, slice(0, 128))
    upval = pltpu.roll(gate, 64, 1)
    sigma = jax.nn.sigmoid(gate)
    hidden = gate * sigma * upval
    hidden = jnp.where(low[0:64], hidden[0:64], pltpu.roll(hidden[64:128], 64, 1))
    dcat[zh, 128:192] = hidden.astype(bf16)
    c_h = gather(1)
    folded = summed(1, slice(128, 192))
    dhidden = jnp.concatenate([folded, pltpu.roll(folded, 64, 1)], axis=0)
    dgate = dhidden * upval * sigma * (1.0 + gate * (1.0 - sigma))
    dup = dhidden * gate * sigma
    dcat[zh, 0:128] = jnp.where(low, dgate, pltpu.roll(dup, 64, 1)).astype(bf16)
    c_g = gather(0)
    c_h = c_h[2:] + pass_on(1, c_h)
    c_g = c_g[2:] + pass_on(0, c_g)

    lo, hi = pl.ds(0, 2), pl.ds(2, 2)
    wide, down_rows = pl.ds(0, 80), pl.ds(80, 40)

    def store(v, rows, values):
        for n in range(4):
            gbuf[v, (n + 4 - z) % 4, rows] = values[n]

    arrived(*c_h)
    low = low_lanes(256)
    folded = dcat[:, 128:192, :].reshape(256, 128).astype(f32)
    early = jnp.where(low, folded, 0.0).astype(bf16).reshape(4, 64, 128)
    late = jnp.where(low, pltpu.roll(folded, 64, 1), 0.0).astype(bf16).reshape(4, 64, 128)
    d2 = jnp.concatenate([early, late], axis=1).reshape(512, 128)

    def backward2(v):
        p2 = jnp.dot(featT[1, v], d2, preferred_element_type=f32).reshape(4, 80, 128)
        rest = pltpu.roll(p2[:, 40:80].reshape(160, 128), 64, 1).reshape(4, 40, 128)
        store(v, down_rows, p2[:, 0:40] + rest)

    backward2(flip(y2))
    h_o = [
        put(gbuf.at[flip(y2), lo, down_rows], gy_half.at[lo, down_rows], up),
        put(gbuf.at[flip(y2), hi, down_rows], gy_half.at[hi, down_rows], down),
    ]
    backward2(flip(yu))
    backward2(flip(yd))
    h_d = [
        put(gbuf.at[flip(yu), hi, down_rows], gy_full.at[0, hi, down_rows], up),
        put(gbuf.at[flip(yd), lo, down_rows], gy_full.at[1, lo, down_rows], down),
    ]
    backward2(flip(y))

    arrived(*c_g)
    d01 = dcat[:, 0:128, :].reshape(512, 128)

    def backward01(v):
        p01 = jnp.dot(featT[0, v], d01, preferred_element_type=f32)
        store(v, wide, p01.reshape(4, 80, 128))

    backward01(flip(y2))
    c_o = [
        put(gbuf.at[flip(y2), k, wide], gy_half.at[k, wide], up if k < 2 else down)
        for k in range(4)
    ]
    backward01(flip(yu))
    c_d = [put(gbuf.at[flip(yu), hi, wide], gy_full.at[0, hi, wide], up)]
    backward01(flip(yd))
    c_d.append(put(gbuf.at[flip(yd), lo, wide], gy_full.at[1, lo, wide], down))
    arrived(h_o[0])
    gbuf[flip(yu), lo, down_rows] += gy_half[lo, down_rows]
    h_d.append(put(gbuf.at[flip(yu), lo, down_rows], gy_full.at[0, lo, down_rows], up))
    arrived(h_o[1])
    gbuf[flip(yd), hi, down_rows] += gy_half[hi, down_rows]
    h_d.append(put(gbuf.at[flip(yd), hi, down_rows], gy_full.at[1, hi, down_rows], down))
    backward01(flip(y))
    c_f = [None] * 4
    for k in (1, 2, 3, 0):
        arrived(c_o[k])
        v = flip(yu) if k < 2 else flip(yd)
        gbuf[v, k, wide] += gy_half[k, wide]
        dst = gy_full.at[k // 2, k, wide]
        c_f[k] = put(gbuf.at[v, k, wide], dst, up if k < 2 else down)

    def along(k, rows):
        gline[k, rows] = gbuf[flip(y), k, rows] + gy_full[0, k, rows] + gy_full[1, k, rows]
        if k > 0:
            return put(gline.at[k, rows], gz_in.at[k - 1, rows], skew[k - 1])

    def home(copies, rows):
        arrived(*copies)
        gline[0, rows] += gz_in[0, rows] + gz_in[1, rows] + gz_in[2, rows]
        return put(gline.at[0, rows], gin.at[rows], owners[0])

    arrived(*h_d)
    h_z = [along(k, down_rows) for k in (1, 2, 3, 0)][:3]
    arrived(*c_d)
    c_z = []
    for k in (1, 2, 3, 0):
        arrived(c_f[k])
        c_z.append(along(k, wide))
    c_home = [home(h_z, down_rows), home(c_z[:3], wide)]
    arrived(*c_home)

    g01 = gin[0:80]
    g2 = jnp.concatenate([gin[80:120], pltpu.roll(gin[80:120], 64, 1)], axis=0)
    grads = jnp.concatenate([g01.T, g2.T[0:64]], axis=0).reshape(3, 64, 80)
    fresh = adamw(grads, state[0], state[1], state[2])[2]
    fin[y, x, 0] = shard_block(fresh.reshape(192, 80))

    c_z = [put(fin.at[y, x, 0], fin.at[y, x, 4 - k], line[k - 1]) for k in (1, 2, 3)]
    grads_out[...] = grads

    class Plane:
        def __init__(self, slots):
            self.slots = slots

        def at(self, yy, xx, start=0, size=128):
            return fin.at[yy, xx, self.slots, pl.ds(start, size)]

        def begin(self):
            a, b = self.at(y, x, 0, 64), self.at(y, x, 64, 64)
            self.ax = [share(a, to) for to in (right, left, across_x)]
            self.by = [share(b, to) for to in (up, down, across_y)]
            self.own = [share(a, up), share(b, right), share(a, down), share(b, left)]

        def turn(self):
            self.a, self.b = [], []
            for n, (xx, yy) in enumerate(((xd, yd), (xu, yu), (x2, y2))):
                arrived(self.ax[n])
                self.a.append([share(self.at(y, xx, 0, 64), to) for to in (up, down)])
                arrived(self.by[n])
                self.b.append([share(self.at(yy, x, 64, 64), to) for to in (right, left)])

        def forward(self):
            self.last = []
            au, br, ad, bl = self.own
            pairs = [(x, y, (au, ad), (br, bl))]
            pairs += zip((xd, xu, x2), (yd, yu, y2), self.a, self.b)
            for xx, yy, a, b in pairs:
                arrived(a[0])
                self.last.append(share(self.at(yd, xx, 0, 32), up))
                arrived(b[0])
                self.last.append(share(self.at(yy, xd, 64, 32), right))
                arrived(a[1])
                self.last.append(share(self.at(yu, xx, 32, 32), down))
                arrived(b[1])
                self.last.append(share(self.at(yy, xu, 96, 32), left))

        def forward_whole(self):
            au, br, ad, bl = self.own
            arrived(au, *(a[0] for a in self.a))
            self.last = [share(fin.at[yd, :, self.slots, pl.ds(0, 32)], up)]
            arrived(br, *(b[0] for b in self.b))
            self.last.append(share(fin.at[:, xd, self.slots, pl.ds(64, 32)], right))
            arrived(ad, *(a[1] for a in self.a))
            self.last.append(share(fin.at[yu, :, self.slots, pl.ds(32, 32)], down))
            arrived(bl, *(b[1] for b in self.b))
            self.last.append(share(fin.at[:, xu, self.slots, pl.ds(96, 32)], left))

        def end(self):
            arrived(*self.last)

    def unpack(r):
        n = (z + r) % 4
        columns = pl.ds(pl.multiple_of(n * 1280, 128), 1280)
        both = fin[:, :, r, 0:80, :].reshape(1280, 128).T
        weights_out[0, :, columns] = both[0:64]
        weights_out[1, :, columns] = both[64:128]
        folded = fin[:, :, r, 80:128, :].reshape(768, 128).astype(f32)
        rest = pltpu.roll(folded, 64, 1).reshape(16, 48, 128)[:, 0:32]
        third = jnp.concatenate([folded.reshape(16, 48, 128), rest], axis=1)
        weights_out[2, :, columns] = third.reshape(1280, 128).astype(bf16).T[0:64]

    near, far = Plane(pl.ds(0, 1)), Plane(pl.ds(1, 3))
    near.begin()
    near.turn()
    arrived(*c_z)
    far.begin()
    far.turn()
    near.forward_whole()
    far.forward()
    near.end()
    unpack(0)
    far.end()
    for r in (1, 2, 3):
        unpack(r)
    finish()


def local(inputs, upstream, master, moment_one, moment_two):
    hbm = pl.BlockSpec(memory_space=pltpu.HBM)
    vmem = pl.BlockSpec(memory_space=pltpu.VMEM)
    operands = (inputs, upstream, master, moment_one, moment_two)
    operands = [pltpu.with_memory_space_constraint(a, pltpu.HBM) for a in operands]
    grads, weights = pl.pallas_call(
        kernel,
        out_shape=(pltpu.VMEM((3, 64, 80), f32), pltpu.VMEM((3, 64, 5120), bf16)),
        in_specs=[hbm] * 5,
        out_specs=(vmem,) * 2,
        scratch_shapes=[
            pltpu.VMEM((2, 4, 2, 128, 640), bf16),
            pltpu.VMEM((3, 3, 64, 80), f32),
            pltpu.VMEM((128, 128), bf16),
            pltpu.VMEM((4, 4, 128, 128), bf16),
            pltpu.VMEM((4, 192, 128), f32),
            pltpu.VMEM((192, 128), f32),
            pltpu.VMEM((2, 192, 128), f32),
            pltpu.VMEM((4, 192, 128), bf16),
            pltpu.VMEM((2, 4, 320, 512), bf16),
            pltpu.VMEM((4, 4, 120, 128), f32),
            pltpu.VMEM((4, 120, 128), f32),
            pltpu.VMEM((2, 4, 120, 128), f32),
            pltpu.VMEM((4, 120, 128), f32),
            pltpu.VMEM((3, 120, 128), f32),
            pltpu.VMEM((120, 128), f32),
            pltpu.VMEM((4, 4, 4, 128, 128), bf16),
            pltpu.SemaphoreType.DMA((N_COPIES,)),
            pltpu.SemaphoreType.DMA((N_COPIES,)),
            pltpu.SemaphoreType.DMA((5,)),
        ],
        compiler_params=pltpu.CompilerParams(
            collective_id=0, has_side_effects=True, vmem_limit_bytes=44 * 2**20
        ),
        cost_estimate=pl.CostEstimate(
            flops=503316480, bytes_accessed=8000000, transcendentals=8192
        ),
        name="fused_step",
    )(*operands)
    first, second, fresh = adamw(grads, master, moment_one, moment_two)
    return fresh, first, second, weights


def solution(mesh):
    owned = P(None, "mp", "dp")
    return jax.shard_map(
        local,
        mesh=mesh,
        in_specs=(P("dp", "mp"), P("dp", "mp"), owned, owned, owned),
        out_specs=(owned, owned, owned, P(None, "mp", None)),
        check_vma=False,
    )
```

```python
import jax
import jax.numpy as jnp
from jax import lax
from jax.experimental import pallas as pl
from jax.experimental.pallas import tpu as pltpu
from jax.sharding import PartitionSpec as P

beta_one = 0.9
beta_two = 0.95
learn_rate = 0.0003
decay_rate = 0.1
eps_small = 1e-08
corr_one = 1.0 - 0.9**40
corr_two = 1.0 - 0.95**40

MESH = pl.DeviceIdType.MESH
f32 = jnp.float32
bf16 = jnp.bfloat16
N_COPIES = 208


def adamw(grads, master, moment_one, moment_two):
    first = beta_one * moment_one + (1.0 - beta_one) * grads
    second = beta_two * moment_two + (1.0 - beta_two) * grads * grads
    update = first / corr_one / (jnp.sqrt(second / corr_two) + eps_small)
    return first, second, master - learn_rate * (update + decay_rate * master)


def kernel(
    inputs_hbm, upstream_hbm, master_hbm, moment_one_hbm, moment_two_hbm,
    fresh_out, first_out, second_out, weights_out,
    feats, state, wown, wbuf, quarter, rs_half, rs_full, dcat,
    featT, gbuf, gy_half, gy_full, gline, gz_in, gin, fin,
    send_sems, recv_sems, load_sems,
):
    i, j = lax.axis_index("dp"), lax.axis_index("mp")
    z, y, x = i // 16, (i // 4) % 4, i % 4
    zh, core = j // 2, j % 2

    def dev(zh=zh, core=core, z=z, y=y, x=x):
        return (z * 16 + y * 4 + x, zh * 2 + core)

    flip = lambda v: v + 1 - 2 * (v % 2)
    xu, xd, x2 = (x + 1) % 4, (x + 3) % 4, (x + 2) % 4
    yu, yd, y2 = (y + 1) % 4, (y + 3) % 4, (y + 2) % 4
    zu, zd, z2 = (zh + 1) % 4, (zh + 3) % 4, (zh + 2) % 4
    right, left, up, down = dev(x=xu), dev(x=xd), dev(y=yu), dev(y=yd)
    across_x, across_y = dev(x=x2), dev(y=y2)
    line = [dev(z=(z + k) % 4) for k in (1, 2, 3)]
    skew = [dev(z=(z + k) % 4, x=(x + k) % 4) for k in (1, 2, 3)]
    above, below = dev(zh=zu), dev(zh=zd)
    mate = dev(core=1 - core)
    holders = [
        dev(zh=z, z=(x + m) % 4, y=flip(y), x=(zh + x + m) % 4) for m in range(4)
    ]
    owners = [
        dev(zh=(x + 4 - z) % 4, z=zh, y=flip(y), x=(z + 4 - m) % 4) for m in range(4)
    ]

    started = []

    def put(src, dst, to):
        k = len(started)
        copy = pltpu.make_async_remote_copy(
            src_ref=src, dst_ref=dst, send_sem=send_sems.at[k], recv_sem=recv_sems.at[k],
            device_id=to, device_id_type=MESH,
        )
        copy.start()
        started.append(copy)
        return copy

    def share(ref, to):
        return put(ref, ref, to)

    def arrived(*copies):
        for copy in copies:
            copy.wait_recv()

    def finish():
        for copy in started:
            copy.wait_send()

    barrier = pltpu.get_barrier_semaphore()
    greeted = [
        *holders, *owners, above, below, *line, *skew,
        right, left, up, down, across_x, across_y, mate,
    ]
    for other in greeted:
        pl.semaphore_signal(barrier, inc=1, device_id=other, device_id_type=MESH)

    loads = [
        pltpu.make_async_copy(src, dst, load_sems.at[k])
        for k, (src, dst) in enumerate([
            (master_hbm, state.at[0]),
            (inputs_hbm, feats.at[0, 0, core]),
            (upstream_hbm, feats.at[1, 0, core]),
            (moment_one_hbm, state.at[1]),
            (moment_two_hbm, state.at[2]),
        ])
    ]
    for load in loads:
        load.start()

    def low_lanes(n):
        return lax.broadcasted_iota(jnp.int32, (n, 128), 1) < 64

    def shard_block(rows):
        down_cols = jnp.concatenate([rows[128:192], jnp.zeros((64, 80), f32)], axis=0).T
        rest = jnp.concatenate([down_cols[48:80], jnp.zeros((16, 128), f32)], axis=0)
        folded = down_cols[0:48] + pltpu.roll(rest, 64, 1)
        return jnp.concatenate([rows[0:128].T, folded], axis=0).astype(bf16)

    loads[0].wait()
    wown[...] = shard_block(state[0].reshape(192, 80))
    for load in loads[1:]:
        load.wait()

    pl.semaphore_wait(barrier, len(greeted))

    gate_up, down_part = pl.ds(0, 80), pl.ds(80, 48)
    c_w = [
        [put(wown.at[rows], wbuf.at[y, x, rows], to) for to in holders]
        for rows in (gate_up, down_part)
    ]
    own = [feats.at[n, 0, core] for n in (0, 1)]
    c_r, c_l = [], []
    for n in (0, 1):
        c_r.append(put(own[n], feats.at[n, 3, core], right))
        c_l.append(put(own[n], feats.at[n, 1, core], left))
    c_m = [[share(own[n], mate)] for n in (0, 1)]
    c_y = [[], []]

    def spread(n, m):
        arrived(c_w[n][m])
        piece = wbuf.at[flip(y), (z + 4 - m) % 4, (gate_up, down_part)[n]]
        c_y[n].extend(share(piece, to) for to in (up, down, across_y))

    arrived(c_r[0])
    c_r2 = put(feats.at[0, 3, core], feats.at[0, 2, core], right)
    c_m[0].append(share(feats.at[0, 3, core], mate))
    arrived(c_l[0])
    c_m[0].append(share(feats.at[0, 1, core], mate))
    for m in range(4):
        spread(0, m)
    arrived(c_l[1])
    c_l2 = put(feats.at[1, 1, core], feats.at[1, 2, core], left)
    c_m[1].append(share(feats.at[1, 1, core], mate))
    for m in range(4):
        spread(1, m)
    arrived(c_r2)
    c_m[0].append(share(feats.at[0, 2, core], mate))
    arrived(c_r[1])
    c_m[1].append(share(feats.at[1, 3, core], mate))
    arrived(*c_m[0], *c_y[0])

    w01 = wbuf[:, :, 0:80, :].reshape(1280, 128)
    w01 = (w01[0:640], w01[640:1280])

    def forward01(q):
        p01 = jnp.dot(feats[0, q, 0], w01[0], preferred_element_type=f32)
        p01 += jnp.dot(feats[0, q, 1], w01[1], preferred_element_type=f32)
        quarter[q, 0:128] = p01

    def forward2(q):
        p2 = jnp.dot(feats[1, q, 0], w2[0], preferred_element_type=f32)
        p2 += jnp.dot(feats[1, q, 1], w2[1], preferred_element_type=f32)
        quarter[q, 128:192] = p2[0:64] + pltpu.roll(p2[64:128], 64, 1)

    lo, hi = (pl.ds(0, 64), pl.ds(128, 32)), (pl.ds(64, 64), pl.ds(160, 32))

    def opposite(n):
        return (
            put(quarter.at[z2, lo[n]], rs_half.at[lo[n]], above),
            put(quarter.at[z2, hi[n]], rs_half.at[hi[n]], below),
        )

    def direct(n):
        return (
            put(quarter.at[zu, hi[n]], rs_full.at[0, hi[n]], above),
            put(quarter.at[zd, lo[n]], rs_full.at[1, lo[n]], below),
        )

    def onward(n, c_a, c_b):
        arrived(c_a)
        quarter[zu, lo[n]] += rs_half[lo[n]]
        c_up = put(quarter.at[zu, lo[n]], rs_full.at[0, lo[n]], above)
        arrived(c_b)
        quarter[zd, hi[n]] += rs_half[hi[n]]
        return c_up, put(quarter.at[zd, hi[n]], rs_full.at[1, hi[n]], below)

    forward01(z2)
    c_o1 = opposite(0)
    forward01(zu)
    forward01(zd)
    arrived(c_l2)
    c_m[1].append(share(feats.at[1, 2, core], mate))
    arrived(*c_m[1], *c_y[1])
    folded = wbuf[:, :, 80:128, :].reshape(768, 128).astype(f32)
    low = low_lanes(768)
    first_rows = jnp.where(low, folded, 0.0).astype(bf16).reshape(16, 48, 128)
    last_rows = jnp.where(low, pltpu.roll(folded, 64, 1), 0.0).astype(bf16).reshape(16, 48, 128)
    w2 = jnp.concatenate([first_rows, last_rows[:, 0:32]], axis=1).reshape(1280, 128)
    w2 = (w2[0:640], w2[640:1280])
    forward2(z2)
    c_o2 = opposite(1)
    c_d = [direct(0)]
    forward2(zu)
    forward2(zd)
    c_d.append(direct(1))
    forward01(zh)
    forward2(zh)
    c_d[0] += onward(0, *c_o1)
    c_d[1] += onward(1, *c_o2)
    for n in (0, 1):
        for q in range(4):
            for d in (0, 1):
                block = feats[n, q, d].T.reshape(2, 320, 128)
                featT[n, 2 * d : 2 * d + 2, :, 128 * q : 128 * q + 128] = block

    def summed(n, rows):
        arrived(*c_d[n])
        return quarter[zh, rows] + rs_full[0, rows] + rs_full[1, rows]

    def gather(n):
        mine, a, b = dcat.at[zh], lo[n], hi[n]
        pairs = ((a, above), (b, below), (b, above), (a, below))
        return [share(mine.at[rows], to) for rows, to in pairs]

    def pass_on(n, copies):
        arrived(copies[0])
        c_a = share(dcat.at[zd, lo[n]], above)
        arrived(copies[1])
        return [c_a, share(dcat.at[zu, hi[n]], below)]

    low = low_lanes(128)
    gate = summed(0, slice(0, 128))
    upval = pltpu.roll(gate, 64, 1)
    sigma = jax.nn.sigmoid(gate)
    hidden = gate * sigma * upval
    hidden = jnp.where(low[0:64], hidden[0:64], pltpu.roll(hidden[64:128], 64, 1))
    dcat[zh, 128:192] = hidden.astype(bf16)
    c_h = gather(1)
    folded = summed(1, slice(128, 192))
    dhidden = jnp.concatenate([folded, pltpu.roll(folded, 64, 1)], axis=0)
    dgate = dhidden * upval * sigma * (1.0 + gate * (1.0 - sigma))
    dup = dhidden * gate * sigma
    dcat[zh, 0:128] = jnp.where(low, dgate, pltpu.roll(dup, 64, 1)).astype(bf16)
    c_g = gather(0)
    c_h = c_h[2:] + pass_on(1, c_h)
    c_g = c_g[2:] + pass_on(0, c_g)

    lo, hi = pl.ds(0, 2), pl.ds(2, 2)
    wide, down_rows = pl.ds(0, 80), pl.ds(80, 40)

    def store(v, rows, values):
        for n in range(4):
            gbuf[v, (n + 4 - z) % 4, rows] = values[n]

    arrived(*c_h)
    low = low_lanes(256)
    folded = dcat[:, 128:192, :].reshape(256, 128).astype(f32)
    early = jnp.where(low, folded, 0.0).astype(bf16).reshape(4, 64, 128)
    late = jnp.where(low, pltpu.roll(folded, 64, 1), 0.0).astype(bf16).reshape(4, 64, 128)
    d2 = jnp.concatenate([early, late], axis=1).reshape(512, 128)

    def backward2(v):
        p2 = jnp.dot(featT[1, v], d2, preferred_element_type=f32).reshape(4, 80, 128)
        rest = pltpu.roll(p2[:, 40:80].reshape(160, 128), 64, 1).reshape(4, 40, 128)
        store(v, down_rows, p2[:, 0:40] + rest)

    backward2(flip(y2))
    h_o = [
        put(gbuf.at[flip(y2), lo, down_rows], gy_half.at[lo, down_rows], up),
        put(gbuf.at[flip(y2), hi, down_rows], gy_half.at[hi, down_rows], down),
    ]
    backward2(flip(yu))
    backward2(flip(yd))
    h_d = [
        put(gbuf.at[flip(yu), hi, down_rows], gy_full.at[0, hi, down_rows], up),
        put(gbuf.at[flip(yd), lo, down_rows], gy_full.at[1, lo, down_rows], down),
    ]
    backward2(flip(y))

    arrived(*c_g)
    d01 = dcat[:, 0:128, :].reshape(512, 128)

    def backward01(v):
        p01 = jnp.dot(featT[0, v], d01, preferred_element_type=f32)
        store(v, wide, p01.reshape(4, 80, 128))

    backward01(flip(y2))
    c_o = [
        put(gbuf.at[flip(y2), k, wide], gy_half.at[k, wide], up if k < 2 else down)
        for k in range(4)
    ]
    backward01(flip(yu))
    c_d = [put(gbuf.at[flip(yu), hi, wide], gy_full.at[0, hi, wide], up)]
    backward01(flip(yd))
    c_d.append(put(gbuf.at[flip(yd), lo, wide], gy_full.at[1, lo, wide], down))
    arrived(h_o[0])
    gbuf[flip(yu), lo, down_rows] += gy_half[lo, down_rows]
    h_d.append(put(gbuf.at[flip(yu), lo, down_rows], gy_full.at[0, lo, down_rows], up))
    arrived(h_o[1])
    gbuf[flip(yd), hi, down_rows] += gy_half[hi, down_rows]
    h_d.append(put(gbuf.at[flip(yd), hi, down_rows], gy_full.at[1, hi, down_rows], down))
    backward01(flip(y))
    c_f = [None] * 4
    for k in (1, 2, 3, 0):
        arrived(c_o[k])
        v = flip(yu) if k < 2 else flip(yd)
        gbuf[v, k, wide] += gy_half[k, wide]
        dst = gy_full.at[k // 2, k, wide]
        c_f[k] = put(gbuf.at[v, k, wide], dst, up if k < 2 else down)

    def along(k, rows):
        gline[k, rows] = gbuf[flip(y), k, rows] + gy_full[0, k, rows] + gy_full[1, k, rows]
        if k > 0:
            return put(gline.at[k, rows], gz_in.at[k - 1, rows], skew[k - 1])

    def home(copies, rows):
        arrived(*copies)
        gline[0, rows] += gz_in[0, rows] + gz_in[1, rows] + gz_in[2, rows]
        return put(gline.at[0, rows], gin.at[rows], owners[0])

    arrived(*h_d)
    h_z = [along(k, down_rows) for k in (1, 2, 3, 0)][:3]
    arrived(*c_d)
    c_z = []
    for k in (1, 2, 3, 0):
        arrived(c_f[k])
        c_z.append(along(k, wide))
    c_home = [home(h_z, down_rows), home(c_z[:3], wide)]
    arrived(*c_home)

    g01 = gin[0:80]
    g2 = jnp.concatenate([gin[80:120], pltpu.roll(gin[80:120], 64, 1)], axis=0)
    grads = jnp.concatenate([g01.T, g2.T[0:64]], axis=0).reshape(3, 64, 80)
    first, second, fresh = adamw(grads, state[0], state[1], state[2])
    fin[y, x, 0] = shard_block(fresh.reshape(192, 80))

    c_z = [put(fin.at[y, x, 0], fin.at[y, x, 4 - k], line[k - 1]) for k in (1, 2, 3)]
    fresh_out[...] = fresh
    first_out[...] = first
    second_out[...] = second

    class Plane:
        def __init__(self, slots):
            self.slots = slots

        def at(self, yy, xx, start=0, size=128):
            return fin.at[yy, xx, self.slots, pl.ds(start, size)]

        def begin(self):
            a, b = self.at(y, x, 0, 64), self.at(y, x, 64, 64)
            self.ax = [share(a, to) for to in (right, left, across_x)]
            self.by = [share(b, to) for to in (up, down, across_y)]
            self.own = [share(a, up), share(b, right), share(a, down), share(b, left)]

        def turn(self):
            self.a, self.b = [], []
            for n, (xx, yy) in enumerate(((xd, yd), (xu, yu), (x2, y2))):
                arrived(self.ax[n])
                self.a.append([share(self.at(y, xx, 0, 64), to) for to in (up, down)])
                arrived(self.by[n])
                self.b.append([share(self.at(yy, x, 64, 64), to) for to in (right, left)])

        def forward(self):
            self.last = []
            au, br, ad, bl = self.own
            pairs = [(x, y, (au, ad), (br, bl))]
            pairs += zip((xd, xu, x2), (yd, yu, y2), self.a, self.b)
            for xx, yy, a, b in pairs:
                arrived(a[0])
                self.last.append(share(self.at(yd, xx, 0, 32), up))
                arrived(b[0])
                self.last.append(share(self.at(yy, xd, 64, 32), right))
                arrived(a[1])
                self.last.append(share(self.at(yu, xx, 32, 32), down))
                arrived(b[1])
                self.last.append(share(self.at(yy, xu, 96, 32), left))

        def forward_whole(self):
            au, br, ad, bl = self.own
            arrived(au, *(a[0] for a in self.a))
            self.last = [share(fin.at[yd, :, self.slots, pl.ds(0, 32)], up)]
            arrived(br, *(b[0] for b in self.b))
            self.last.append(share(fin.at[:, xd, self.slots, pl.ds(64, 32)], right))
            arrived(ad, *(a[1] for a in self.a))
            self.last.append(share(fin.at[yu, :, self.slots, pl.ds(32, 32)], down))
            arrived(bl, *(b[1] for b in self.b))
            self.last.append(share(fin.at[:, xu, self.slots, pl.ds(96, 32)], left))

        def end(self):
            arrived(*self.last)

    def unpack(r):
        n = (z + r) % 4
        columns = pl.ds(pl.multiple_of(n * 1280, 128), 1280)
        both = fin[:, :, r, 0:80, :].reshape(1280, 128).T
        weights_out[0, :, columns] = both[0:64]
        weights_out[1, :, columns] = both[64:128]
        folded = fin[:, :, r, 80:128, :].reshape(768, 128).astype(f32)
        rest = pltpu.roll(folded, 64, 1).reshape(16, 48, 128)[:, 0:32]
        third = jnp.concatenate([folded.reshape(16, 48, 128), rest], axis=1)
        weights_out[2, :, columns] = third.reshape(1280, 128).astype(bf16).T[0:64]

    near, far = Plane(pl.ds(0, 1)), Plane(pl.ds(1, 3))
    near.begin()
    near.turn()
    arrived(*c_z)
    far.begin()
    far.turn()
    near.forward_whole()
    far.forward()
    near.end()
    unpack(0)
    far.end()
    for r in (1, 2, 3):
        unpack(r)
    finish()


def write_back(*refs):
    sources, targets, sems = refs[0:4], refs[4:8], refs[8]
    copies = [
        pltpu.make_async_copy(sources[k], targets[k], sems.at[k]) for k in (3, 0, 1, 2)
    ]
    for copy in copies:
        copy.start()
    for copy in copies:
        copy.wait()


def local(inputs, upstream, master, moment_one, moment_two):
    hbm = pl.BlockSpec(memory_space=pltpu.HBM)
    vmem = pl.BlockSpec(memory_space=pltpu.VMEM)
    operands = (inputs, upstream, master, moment_one, moment_two)
    operands = [pltpu.with_memory_space_constraint(a, pltpu.HBM) for a in operands]
    results = pl.pallas_call(
        kernel,
        out_shape=(*(pltpu.VMEM((3, 64, 80), f32),) * 3, pltpu.VMEM((3, 64, 5120), bf16)),
        in_specs=[hbm] * 5,
        out_specs=(vmem,) * 4,
        scratch_shapes=[
            pltpu.VMEM((2, 4, 2, 128, 640), bf16),
            pltpu.VMEM((3, 3, 64, 80), f32),
            pltpu.VMEM((128, 128), bf16),
            pltpu.VMEM((4, 4, 128, 128), bf16),
            pltpu.VMEM((4, 192, 128), f32),
            pltpu.VMEM((192, 128), f32),
            pltpu.VMEM((2, 192, 128), f32),
            pltpu.VMEM((4, 192, 128), bf16),
            pltpu.VMEM((2, 4, 320, 512), bf16),
            pltpu.VMEM((4, 4, 120, 128), f32),
            pltpu.VMEM((4, 120, 128), f32),
            pltpu.VMEM((2, 4, 120, 128), f32),
            pltpu.VMEM((4, 120, 128), f32),
            pltpu.VMEM((3, 120, 128), f32),
            pltpu.VMEM((120, 128), f32),
            pltpu.VMEM((4, 4, 4, 128, 128), bf16),
            pltpu.SemaphoreType.DMA((N_COPIES,)),
            pltpu.SemaphoreType.DMA((N_COPIES,)),
            pltpu.SemaphoreType.DMA((5,)),
        ],
        compiler_params=pltpu.CompilerParams(
            collective_id=0, has_side_effects=True, vmem_limit_bytes=44 * 2**20
        ),
        cost_estimate=pl.CostEstimate(
            flops=503316480, bytes_accessed=8000000, transcendentals=8192
        ),
        name="fused_step",
    )(*operands)
    results = [pltpu.with_memory_space_constraint(a, pltpu.VMEM) for a in results]
    return pl.pallas_call(
        write_back,
        out_shape=tuple(jax.ShapeDtypeStruct(a.shape, a.dtype) for a in results),
        in_specs=[vmem] * 4,
        out_specs=(hbm,) * 4,
        scratch_shapes=[pltpu.SemaphoreType.DMA((4,))],
        cost_estimate=pl.CostEstimate(flops=0, bytes_accessed=4500000, transcendentals=0),
        name="write_back",
    )(*results)


def solution(mesh):
    owned = P(None, "mp", "dp")
    return jax.shard_map(
        local,
        mesh=mesh,
        in_specs=(P("dp", "mp"), P("dp", "mp"), owned, owned, owned),
        out_specs=(owned, owned, owned, P(None, "mp", None)),
        check_vma=False,
    )
```

```python
import jax
import jax.numpy as jnp
from jax import lax
from jax.experimental import pallas as pl
from jax.experimental.pallas import tpu as pltpu
from jax.sharding import PartitionSpec as P

beta_one = 0.9
beta_two = 0.95
learn_rate = 0.0003
decay_rate = 0.1
eps_small = 1e-08
corr_one = 1.0 - 0.9**40
corr_two = 1.0 - 0.95**40

MESH = pl.DeviceIdType.MESH
f32 = jnp.float32
bf16 = jnp.bfloat16
N_COPIES = 208


def adamw(grads, master, moment_one, moment_two):
    first = beta_one * moment_one + (1.0 - beta_one) * grads
    second = beta_two * moment_two + (1.0 - beta_two) * grads * grads
    update = first / corr_one / (jnp.sqrt(second / corr_two) + eps_small)
    return first, second, master - learn_rate * (update + decay_rate * master)


def kernel(
    inputs_hbm, upstream_hbm, master_hbm, moment_one_hbm, moment_two_hbm,
    fresh_out, first_out, second_out, weights_out,
    feats, state, wown, wbuf, quarter, rs_half, rs_full, dcat,
    featT, gbuf, gy_half, gy_full, gline, gz_in, gin, fin,
    send_sems, recv_sems, load_sems,
):
    i, j = lax.axis_index("dp"), lax.axis_index("mp")
    z, y, x = i // 16, (i // 4) % 4, i % 4
    zh, core = j // 2, j % 2

    def dev(zh=zh, core=core, z=z, y=y, x=x):
        return (z * 16 + y * 4 + x, zh * 2 + core)

    flip = lambda v: v + 1 - 2 * (v % 2)
    xu, xd, x2 = (x + 1) % 4, (x + 3) % 4, (x + 2) % 4
    yu, yd, y2 = (y + 1) % 4, (y + 3) % 4, (y + 2) % 4
    zu, zd, z2 = (zh + 1) % 4, (zh + 3) % 4, (zh + 2) % 4
    right, left, up, down = dev(x=xu), dev(x=xd), dev(y=yu), dev(y=yd)
    across_x, across_y = dev(x=x2), dev(y=y2)
    line = [dev(z=(z + k) % 4) for k in (1, 2, 3)]
    skew = [dev(z=(z + k) % 4, x=(x + k) % 4) for k in (1, 2, 3)]
    above, below = dev(zh=zu), dev(zh=zd)
    mate = dev(core=1 - core)
    holders = [
        dev(zh=z, z=(x + m) % 4, y=flip(y), x=(zh + x + m) % 4) for m in range(4)
    ]
    owners = [
        dev(zh=(x + 4 - z) % 4, z=zh, y=flip(y), x=(z + 4 - m) % 4) for m in range(4)
    ]

    started = []

    def put(src, dst, to):
        k = len(started)
        copy = pltpu.make_async_remote_copy(
            src_ref=src, dst_ref=dst, send_sem=send_sems.at[k], recv_sem=recv_sems.at[k],
            device_id=to, device_id_type=MESH,
        )
        copy.start()
        started.append(copy)
        return copy

    def share(ref, to):
        return put(ref, ref, to)

    def arrived(*copies):
        for copy in copies:
            copy.wait_recv()

    def finish():
        for copy in started:
            copy.wait_send()

    barrier = pltpu.get_barrier_semaphore()
    greeted = [
        *owners, *holders, above, below, *line, *skew,
        right, left, up, down, across_x, across_y, mate,
    ]
    for other in greeted:
        pl.semaphore_signal(barrier, inc=1, device_id=other, device_id_type=MESH)

    loads = [
        pltpu.make_async_copy(src, dst, load_sems.at[k])
        for k, (src, dst) in enumerate([
            (master_hbm, state.at[0]),
            (inputs_hbm, feats.at[0, 0, core]),
            (upstream_hbm, feats.at[1, 0, core]),
            (moment_one_hbm, state.at[1]),
            (moment_two_hbm, state.at[2]),
        ])
    ]
    for load in loads:
        load.start()

    def low_lanes(n):
        return lax.broadcasted_iota(jnp.int32, (n, 128), 1) < 64

    def shard_block(rows):
        down_cols = jnp.concatenate([rows[128:192], jnp.zeros((64, 80), f32)], axis=0).T
        rest = jnp.concatenate([down_cols[48:80], jnp.zeros((16, 128), f32)], axis=0)
        folded = down_cols[0:48] + pltpu.roll(rest, 64, 1)
        return jnp.concatenate([rows[0:128].T, folded], axis=0).astype(bf16)

    loads[0].wait()
    wown[...] = shard_block(state[0].reshape(192, 80))
    for load in loads[1:]:
        load.wait()

    pl.semaphore_wait(barrier, len(greeted))

    gate_up, down_part = pl.ds(0, 80), pl.ds(80, 48)
    c_w = [
        [put(wown.at[rows], wbuf.at[y, x, rows], to) for to in holders]
        for rows in (gate_up, down_part)
    ]
    own = [feats.at[n, 0, core] for n in (0, 1)]
    c_r, c_l = [], []
    for n in (0, 1):
        c_r.append(put(own[n], feats.at[n, 3, core], right))
        c_l.append(put(own[n], feats.at[n, 1, core], left))
    c_m = [[share(own[n], mate)] for n in (0, 1)]
    c_y = [[], []]

    def spread(n, m):
        arrived(c_w[n][m])
        piece = wbuf.at[flip(y), (z + 4 - m) % 4, gate_up]
        c_y[n].extend(share(piece, to) for to in (up, down, across_y))

    arrived(c_r[0])
    c_r2 = put(feats.at[0, 3, core], feats.at[0, 2, core], right)
    c_m[0].append(share(feats.at[0, 3, core], mate))
    arrived(c_l[0])
    c_m[0].append(share(feats.at[0, 1, core], mate))
    spread(0, 0)
    spread(0, 1)
    arrived(c_l[1])
    c_l2 = put(feats.at[1, 1, core], feats.at[1, 2, core], left)
    c_m[1].append(share(feats.at[1, 1, core], mate))
    spread(0, 2)
    spread(0, 3)
    arrived(*c_w[1])
    c_y[1] = [share(wbuf.at[flip(y), :, down_part], to) for to in (up, down, across_y)]
    arrived(c_r2)
    c_m[0].append(share(feats.at[0, 2, core], mate))
    arrived(c_r[1])
    c_m[1].append(share(feats.at[1, 3, core], mate))
    arrived(*c_m[0], *c_y[0])

    w01 = wbuf[:, :, 0:80, :].reshape(1280, 128)
    w01 = (w01[0:640], w01[640:1280])

    def forward01(q):
        p01 = jnp.dot(feats[0, q, 0], w01[0], preferred_element_type=f32)
        p01 += jnp.dot(feats[0, q, 1], w01[1], preferred_element_type=f32)
        quarter[q, 0:128] = p01

    def forward2(q):
        p2 = jnp.dot(feats[1, q, 0], w2[0], preferred_element_type=f32)
        p2 += jnp.dot(feats[1, q, 1], w2[1], preferred_element_type=f32)
        quarter[q, 128:192] = p2[0:64] + pltpu.roll(p2[64:128], 64, 1)

    lo, hi = (pl.ds(0, 64), pl.ds(128, 32)), (pl.ds(64, 64), pl.ds(160, 32))

    def opposite(n):
        return (
            put(quarter.at[z2, lo[n]], rs_half.at[lo[n]], above),
            put(quarter.at[z2, hi[n]], rs_half.at[hi[n]], below),
        )

    def direct(n):
        return (
            put(quarter.at[zu, hi[n]], rs_full.at[0, hi[n]], above),
            put(quarter.at[zd, lo[n]], rs_full.at[1, lo[n]], below),
        )

    def onward(n, c_a, c_b):
        arrived(c_a)
        quarter[zu, lo[n]] += rs_half[lo[n]]
        c_up = put(quarter.at[zu, lo[n]], rs_full.at[0, lo[n]], above)
        arrived(c_b)
        quarter[zd, hi[n]] += rs_half[hi[n]]
        return c_up, put(quarter.at[zd, hi[n]], rs_full.at[1, hi[n]], below)

    forward01(z2)
    c_o1 = opposite(0)
    forward01(zu)
    forward01(zd)
    arrived(c_l2)
    c_m[1].append(share(feats.at[1, 2, core], mate))
    arrived(*c_m[1], *c_y[1])
    folded = wbuf[:, :, 80:128, :].reshape(768, 128).astype(f32)
    low = low_lanes(768)
    first_rows = jnp.where(low, folded, 0.0).astype(bf16).reshape(16, 48, 128)
    last_rows = jnp.where(low, pltpu.roll(folded, 64, 1), 0.0).astype(bf16).reshape(16, 48, 128)
    w2 = jnp.concatenate([first_rows, last_rows[:, 0:32]], axis=1).reshape(1280, 128)
    w2 = (w2[0:640], w2[640:1280])
    forward2(z2)
    c_o2 = opposite(1)
    c_d = [direct(0)]
    forward2(zu)
    forward2(zd)
    c_d.append(direct(1))
    forward01(zh)
    forward2(zh)
    c_d[0] += onward(0, *c_o1)
    c_d[1] += onward(1, *c_o2)
    for n in (0, 1):
        for q in range(4):
            for d in (0, 1):
                block = feats[n, q, d].T.reshape(2, 320, 128)
                featT[n, 2 * d : 2 * d + 2, :, 128 * q : 128 * q + 128] = block

    def summed(n, rows):
        arrived(*c_d[n])
        return quarter[zh, rows] + rs_full[0, rows] + rs_full[1, rows]

    def gather(n):
        mine, a, b = dcat.at[zh], lo[n], hi[n]
        pairs = ((a, above), (b, below), (b, above), (a, below))
        return [share(mine.at[rows], to) for rows, to in pairs]

    def pass_on(n, copies):
        arrived(copies[0])
        c_a = share(dcat.at[zd, lo[n]], above)
        arrived(copies[1])
        return [c_a, share(dcat.at[zu, hi[n]], below)]

    low = low_lanes(128)
    gate = summed(0, slice(0, 128))
    upval = pltpu.roll(gate, 64, 1)
    sigma = jax.nn.sigmoid(gate)
    hidden = gate * sigma * upval
    hidden = jnp.where(low[0:64], hidden[0:64], pltpu.roll(hidden[64:128], 64, 1))
    dcat[zh, 128:192] = hidden.astype(bf16)
    c_h = gather(1)
    folded = summed(1, slice(128, 192))
    dhidden = jnp.concatenate([folded, pltpu.roll(folded, 64, 1)], axis=0)
    dgate = dhidden * upval * sigma * (1.0 + gate * (1.0 - sigma))
    dup = dhidden * gate * sigma
    dcat[zh, 0:128] = jnp.where(low, dgate, pltpu.roll(dup, 64, 1)).astype(bf16)
    c_g = gather(0)
    c_h = c_h[2:] + pass_on(1, c_h)
    c_g = c_g[2:] + pass_on(0, c_g)

    lo, hi = pl.ds(0, 2), pl.ds(2, 2)
    wide, down_rows = pl.ds(0, 80), pl.ds(80, 40)

    def store(v, rows, values):
        for n in range(4):
            gbuf[v, (n + 4 - z) % 4, rows] = values[n]

    arrived(*c_h)
    low = low_lanes(256)
    folded = dcat[:, 128:192, :].reshape(256, 128).astype(f32)
    early = jnp.where(low, folded, 0.0).astype(bf16).reshape(4, 64, 128)
    late = jnp.where(low, pltpu.roll(folded, 64, 1), 0.0).astype(bf16).reshape(4, 64, 128)
    d2 = jnp.concatenate([early, late], axis=1).reshape(512, 128)

    def backward2(v):
        p2 = jnp.dot(featT[1, v], d2, preferred_element_type=f32).reshape(4, 80, 128)
        rest = pltpu.roll(p2[:, 40:80].reshape(160, 128), 64, 1).reshape(4, 40, 128)
        store(v, down_rows, p2[:, 0:40] + rest)

    backward2(flip(y2))
    h_o = [
        put(gbuf.at[flip(y2), lo, down_rows], gy_half.at[lo, down_rows], up),
        put(gbuf.at[flip(y2), hi, down_rows], gy_half.at[hi, down_rows], down),
    ]
    backward2(flip(yu))
    backward2(flip(yd))
    h_d = [
        put(gbuf.at[flip(yu), hi, down_rows], gy_full.at[0, hi, down_rows], up),
        put(gbuf.at[flip(yd), lo, down_rows], gy_full.at[1, lo, down_rows], down),
    ]
    backward2(flip(y))

    arrived(*c_g)
    d01 = dcat[:, 0:128, :].reshape(512, 128)

    def backward01(v):
        p01 = jnp.dot(featT[0, v], d01, preferred_element_type=f32)
        store(v, wide, p01.reshape(4, 80, 128))

    backward01(flip(y2))
    c_o = [
        put(gbuf.at[flip(y2), k, wide], gy_half.at[k, wide], up if k < 2 else down)
        for k in range(4)
    ]
    backward01(flip(yu))
    c_d = [put(gbuf.at[flip(yu), hi, wide], gy_full.at[0, hi, wide], up)]
    backward01(flip(yd))
    c_d.append(put(gbuf.at[flip(yd), lo, wide], gy_full.at[1, lo, wide], down))
    arrived(h_o[0])
    gbuf[flip(yu), lo, down_rows] += gy_half[lo, down_rows]
    h_d.append(put(gbuf.at[flip(yu), lo, down_rows], gy_full.at[0, lo, down_rows], up))
    arrived(h_o[1])
    gbuf[flip(yd), hi, down_rows] += gy_half[hi, down_rows]
    h_d.append(put(gbuf.at[flip(yd), hi, down_rows], gy_full.at[1, hi, down_rows], down))
    backward01(flip(y))
    c_f = [None] * 4
    for k in (1, 2, 3, 0):
        arrived(c_o[k])
        v = flip(yu) if k < 2 else flip(yd)
        gbuf[v, k, wide] += gy_half[k, wide]
        dst = gy_full.at[k // 2, k, wide]
        c_f[k] = put(gbuf.at[v, k, wide], dst, up if k < 2 else down)

    def along(k, rows):
        gline[k, rows] = gbuf[flip(y), k, rows] + gy_full[0, k, rows] + gy_full[1, k, rows]
        if k > 0:
            return put(gline.at[k, rows], gz_in.at[k - 1, rows], skew[k - 1])

    def home(copies, rows):
        arrived(*copies)
        gline[0, rows] += gz_in[0, rows] + gz_in[1, rows] + gz_in[2, rows]
        return put(gline.at[0, rows], gin.at[rows], owners[0])

    arrived(*h_d)
    h_z = [along(k, down_rows) for k in (1, 2, 3, 0)][:3]
    arrived(*c_d)
    c_z = []
    for k in (1, 2, 3, 0):
        arrived(c_f[k])
        c_z.append(along(k, wide))
    c_home = [home(h_z, down_rows), home(c_z[:3], wide)]
    arrived(*c_home)

    g01 = gin[0:80]
    g2 = jnp.concatenate([gin[80:120], pltpu.roll(gin[80:120], 64, 1)], axis=0)
    grads = jnp.concatenate([g01.T, g2.T[0:64]], axis=0).reshape(3, 64, 80)
    first, second, fresh = adamw(grads, state[0], state[1], state[2])
    fin[y, x, 0] = shard_block(fresh.reshape(192, 80))

    c_z = [put(fin.at[y, x, 0], fin.at[y, x, 4 - k], line[k - 1]) for k in (1, 2, 3)]
    fresh_out[...] = fresh
    first_out[...] = first
    second_out[...] = second

    class Plane:
        def __init__(self, slots):
            self.slots = slots

        def at(self, yy, xx, start=0, size=128):
            return fin.at[yy, xx, self.slots, pl.ds(start, size)]

        def begin(self):
            a, b = self.at(y, x, 0, 64), self.at(y, x, 64, 64)
            self.ax = [share(a, to) for to in (right, left, across_x)]
            self.by = [share(b, to) for to in (up, down, across_y)]
            self.own = [share(a, up), share(b, right), share(a, down), share(b, left)]

        def turn(self):
            self.a, self.b = [], []
            for n, (xx, yy) in enumerate(((xd, yd), (xu, yu), (x2, y2))):
                arrived(self.ax[n])
                self.a.append([share(self.at(y, xx, 0, 64), to) for to in (up, down)])
                arrived(self.by[n])
                self.b.append([share(self.at(yy, x, 64, 64), to) for to in (right, left)])

        def forward(self):
            self.last = []
            au, br, ad, bl = self.own
            pairs = [(x, y, (au, ad), (br, bl))]
            pairs += zip((xd, xu, x2), (yd, yu, y2), self.a, self.b)
            for xx, yy, a, b in pairs:
                arrived(a[0])
                self.last.append(share(self.at(yd, xx, 0, 32), up))
                arrived(b[0])
                self.last.append(share(self.at(yy, xd, 64, 32), right))
                arrived(a[1])
                self.last.append(share(self.at(yu, xx, 32, 32), down))
                arrived(b[1])
                self.last.append(share(self.at(yy, xu, 96, 32), left))

        def forward_whole(self):
            au, br, ad, bl = self.own
            arrived(au, *(a[0] for a in self.a))
            self.last = [share(fin.at[yd, :, self.slots, pl.ds(0, 32)], up)]
            arrived(br, *(b[0] for b in self.b))
            self.last.append(share(fin.at[:, xd, self.slots, pl.ds(64, 32)], right))
            arrived(ad, *(a[1] for a in self.a))
            self.last.append(share(fin.at[yu, :, self.slots, pl.ds(32, 32)], down))
            arrived(bl, *(b[1] for b in self.b))
            self.last.append(share(fin.at[:, xu, self.slots, pl.ds(96, 32)], left))

        def end(self):
            arrived(*self.last)

    def unpack(r):
        n = (z + r) % 4
        columns = pl.ds(pl.multiple_of(n * 1280, 128), 1280)
        both = fin[:, :, r, 0:80, :].reshape(1280, 128).T
        weights_out[0, :, columns] = both[0:64]
        weights_out[1, :, columns] = both[64:128]
        folded = fin[:, :, r, 80:128, :].reshape(768, 128).astype(f32)
        rest = pltpu.roll(folded, 64, 1).reshape(16, 48, 128)[:, 0:32]
        third = jnp.concatenate([folded.reshape(16, 48, 128), rest], axis=1)
        weights_out[2, :, columns] = third.reshape(1280, 128).astype(bf16).T[0:64]

    near, far = Plane(pl.ds(0, 1)), Plane(pl.ds(1, 3))
    near.begin()
    near.turn()
    arrived(*c_z)
    far.begin()
    far.turn()
    near.forward_whole()
    far.forward()
    near.end()
    unpack(0)
    far.end()
    for r in (1, 2, 3):
        unpack(r)
    finish()


def write_back(*refs):
    sources, targets, sems = refs[0:4], refs[4:8], refs[8]
    copies = [
        pltpu.make_async_copy(sources[k], targets[k], sems.at[k]) for k in (3, 0, 1, 2)
    ]
    for copy in copies:
        copy.start()
    for copy in copies:
        copy.wait()


def local(inputs, upstream, master, moment_one, moment_two):
    hbm = pl.BlockSpec(memory_space=pltpu.HBM)
    vmem = pl.BlockSpec(memory_space=pltpu.VMEM)
    operands = (inputs, upstream, master, moment_one, moment_two)
    operands = [pltpu.with_memory_space_constraint(a, pltpu.HBM) for a in operands]
    results = pl.pallas_call(
        kernel,
        out_shape=(*(pltpu.VMEM((3, 64, 80), f32),) * 3, pltpu.VMEM((3, 64, 5120), bf16)),
        in_specs=[hbm] * 5,
        out_specs=(vmem,) * 4,
        scratch_shapes=[
            pltpu.VMEM((2, 4, 2, 128, 640), bf16),
            pltpu.VMEM((3, 3, 64, 80), f32),
            pltpu.VMEM((128, 128), bf16),
            pltpu.VMEM((4, 4, 128, 128), bf16),
            pltpu.VMEM((4, 192, 128), f32),
            pltpu.VMEM((192, 128), f32),
            pltpu.VMEM((2, 192, 128), f32),
            pltpu.VMEM((4, 192, 128), bf16),
            pltpu.VMEM((2, 4, 320, 512), bf16),
            pltpu.VMEM((4, 4, 120, 128), f32),
            pltpu.VMEM((4, 120, 128), f32),
            pltpu.VMEM((2, 4, 120, 128), f32),
            pltpu.VMEM((4, 120, 128), f32),
            pltpu.VMEM((3, 120, 128), f32),
            pltpu.VMEM((120, 128), f32),
            pltpu.VMEM((4, 4, 4, 128, 128), bf16),
            pltpu.SemaphoreType.DMA((N_COPIES,)),
            pltpu.SemaphoreType.DMA((N_COPIES,)),
            pltpu.SemaphoreType.DMA((5,)),
        ],
        compiler_params=pltpu.CompilerParams(
            collective_id=0, has_side_effects=True, vmem_limit_bytes=44 * 2**20
        ),
        cost_estimate=pl.CostEstimate(
            flops=503316480, bytes_accessed=8000000, transcendentals=8192
        ),
        name="fused_step",
    )(*operands)
    results = [pltpu.with_memory_space_constraint(a, pltpu.VMEM) for a in results]
    return pl.pallas_call(
        write_back,
        out_shape=tuple(jax.ShapeDtypeStruct(a.shape, a.dtype) for a in results),
        in_specs=[vmem] * 4,
        out_specs=(hbm,) * 4,
        scratch_shapes=[pltpu.SemaphoreType.DMA((4,))],
        cost_estimate=pl.CostEstimate(flops=0, bytes_accessed=4500000, transcendentals=0),
        name="write_back",
    )(*results)


def solution(mesh):
    owned = P(None, "mp", "dp")
    return jax.shard_map(
        local,
        mesh=mesh,
        in_specs=(P("dp", "mp"), P("dp", "mp"), owned, owned, owned),
        out_specs=(owned, owned, owned, P(None, "mp", None)),
        check_vma=False,
    )
```
